128 devices in a mesh: group: 8 (over y_lo, x), head: 16 (over y_hi, z, core).
Axes of the slice: x: 4, y: 4 (y_hi: 2, y_lo: 2; y = y_hi * 2 + y_lo), z: 4, core: 2. Of those that a mesh axis runs over, the one named last changes fastest.
Arguments:
- query_rows: bfloat16 [8, 1024, 6144], P('group', 'head'), may hold values from -120 to 120
- key_rows: bfloat16 [8, 1024, 6144], P('group', 'head'), may hold values from -6 to 6
- value_rows: bfloat16 [8, 1024, 6144], P('group', 'head'), may hold values from -6 to 6
- group_order: int32 [8], replicated, may hold values from 0 to 7, each once
- valid_counts: int32 [8], replicated, may hold values from 512 to 1024, as said below
Outputs:
- attended: bfloat16 [8, 1024, 6144], P('group', 'head')
The draws below stay inside these ranges and needn't reach their ends.
Inputs may be any that keep to these rules, and one draw needn't show every extreme that they name: `group_order`: a permutation of the groups. `valid_counts`: one group is full and one holds exactly half of its 1024 slots.
All inputs are finite; a program needn't handle non-finite values.
Results may differ from the reference program's by a relative error of at most 0.006.
Values may be sent and summed in bfloat16 or wider, within the bound.
No kernel may reach another device: no remote copies, remote signals or barrier semaphores. Data moves between devices by JAX's collectives and lax.ppermute only.
A program may use at most 128 MiB of HBM per device.

```python
import jax
import jax.numpy as jnp
from jax import lax

H = 48
HD = 128
TOK = 1024
GROUPS = 8


def shared_keys(key):
    return jnp.clip(jax.random.normal(key, (GROUPS, TOK, H * HD), jnp.float32), -6.0, 6.0)


def draw_key_rows(key, part):
    base = shared_keys(key)
    return base.astype(jnp.bfloat16)


def draw_query_rows(key, part):
    key = jax.random.fold_in(key, 2)
    fresh = jnp.clip(jax.random.normal(key, (GROUPS, TOK, H * HD), jnp.float32), -6.0, 6.0)
    return fresh.astype(jnp.bfloat16)


def draw_valid_counts(key, part):
    key = jax.random.fold_in(key, 5)
    counts = jax.random.randint(key, (GROUPS,), TOK // 2, TOK + 1, jnp.int32)
    chosen = jax.random.permutation(jax.random.fold_in(key, 6), GROUPS)
    slots = jnp.arange(GROUPS, dtype=jnp.int32)
    counts = jnp.where(slots == chosen[0], TOK, counts)
    counts = jnp.where(slots == chosen[1], TOK // 2, counts)
    return counts.astype(jnp.int32)


def levels(own_key, extent, cuts, smallest, high):
    factor_of, own = 1.0, jax.random.fold_in(own_key, 6)
    for dim, parts in cuts:
        draws = jnp.exp(jax.random.uniform(jax.random.fold_in(own, dim), (parts,), jnp.float32, smallest / len(cuts), high / len(cuts)))
        factor_of = factor_of * jnp.repeat(draws, extent[dim] // parts).reshape([-1 if axis == dim else 1 for axis in range(len(extent))])
    return factor_of


def normal_values(own_key, shape, width, most, shards=(), kind=jnp.bfloat16):
    entries = width * jax.random.normal(own_key, shape, jnp.float32)
    if shards:
        entries = entries * levels(own_key, shape, shards, -0.22, 0.18)
    return jnp.clip(entries, -most, most).astype(kind)


def setup_inputs(seed: int = 0) -> dict:
    key_of = jax.random.split(jax.random.key(seed), 6)
    query_rows = draw_query_rows(jax.random.fold_in(key_of[5], 71), 0)
    key_rows = draw_key_rows(jax.random.fold_in(key_of[5], 71), 0)
    value_rows = normal_values(key_of[2], (GROUPS, TOK, H * HD), 1.0, 6.0, ((0, 8), (1, 16)))
    group_order = jax.random.permutation(key_of[3], GROUPS).astype(jnp.int32)
    valid_counts = draw_valid_counts(jax.random.fold_in(key_of[5], 71), 0)
    return dict(query_rows=query_rows, key_rows=key_rows, value_rows=value_rows, group_order=group_order, valid_counts=valid_counts)


def reference(query_rows, key_rows, value_rows, group_order, valid_counts):
    scale = HD ** -0.5
    all_keys = key_rows.reshape(GROUPS * TOK, H, HD).transpose(1, 0, 2)
    all_values = value_rows.reshape(GROUPS * TOK, H, HD).transpose(1, 0, 2)
    key_group = jnp.arange(GROUPS * TOK, dtype=jnp.int32) // TOK
    key_spot = jnp.arange(GROUPS * TOK, dtype=jnp.int32) % TOK
    spots = jnp.arange(TOK, dtype=jnp.int32)
    results = []
    for group in range(GROUPS):
        allowed = (group_order[key_group] < group_order[group]) | (key_group == group)
        allowed = allowed & (key_spot < valid_counts[key_group])
        queries = query_rows[group].reshape(TOK, H, HD).transpose(1, 0, 2)

        def one_head(operands):
            head_queries, head_keys, head_values = operands
            scores = jnp.dot(head_queries, head_keys.T, preferred_element_type=jnp.float32) * scale
            scores = jnp.where(allowed[None, :], scores, jnp.float32(-1e30))
            peak = jnp.max(scores, axis=1, keepdims=True)
            raised = jnp.where(allowed[None, :], jnp.exp(scores - peak), jnp.float32(0.0))
            totals = jnp.sum(raised, axis=1, keepdims=True)
            mixed = jnp.dot(raised.astype(jnp.bfloat16), head_values, preferred_element_type=jnp.float32)
            return mixed / totals

        outputs = lax.map(one_head, (queries, all_keys, all_values))
        outputs = outputs.transpose(1, 0, 2).reshape(TOK, H * HD)
        outputs = jnp.where((spots < valid_counts[group])[:, None], outputs, jnp.float32(0.0))
        results.append(outputs.astype(jnp.bfloat16))
    return jnp.stack(results, axis=0)
```

```python
import functools
import math

import jax
import jax.numpy as jnp
from jax import lax
from jax.experimental import pallas as pl
from jax.experimental.pallas import tpu as pltpu
from jax.sharding import PartitionSpec as P

HD = 128
ROWS = 64
CHUNK = 512
SCALE = HD ** (-0.5)
LOG2E = math.log2(math.e)
LOW, HIGH = 2.0**-80, 2.0**110


def attend_kernel(slots, facts, order, valid, own, other, out, keys, values, total, peak, place, ends):
    parity, active = facts[0], facts[1]
    groups = order.shape[0]
    per_group = own.shape[0] // groups
    slab = per_group * ROWS

    @pl.when(active == 1)
    def _():
        for j in range(groups):
            place[order[j]] = j

        def pack_group(p, start):
            j = place[p]
            blocks = (valid[j] + ROWS - 1) // ROWS
            for core in range(2):
                count = (blocks - core + 1) // 2

                def pack(source):
                    def one(s, carry):
                        left = valid[j] - (2 * s + core) * ROWS
                        at = pl.multiple_of((start + s) * ROWS, ROWS)
                        block_keys = source[j * per_group + s, 1]
                        block_values = source[j * per_group + s, 2]
                        there = lax.broadcasted_iota(jnp.int32, (ROWS, HD), 0) < left
                        first = jnp.broadcast_to(block_keys[0:1, :], (ROWS, HD))
                        keys[pl.ds(at, ROWS), :] = jnp.where(there, block_keys, first)
                        values[pl.ds(at, ROWS), 0:HD] = jnp.where(there, block_values, jnp.zeros_like(block_values))
                        values[pl.ds(at, ROWS), HD : 2 * HD] = jnp.where(there, 1.0, 0.0).astype(jnp.bfloat16)
                        return carry

                    lax.fori_loop(0, count, one, 0)

                @pl.when(parity == core)
                def _():
                    pack(own)

                @pl.when(parity != core)
                def _():
                    pack(other)

                start = start + count
            ends[p] = start
            return start

        last = lax.fori_loop(0, groups, pack_group, 0)
        tail = pl.multiple_of(last * ROWS, ROWS)
        values[pl.ds(tail, CHUNK), :] = jnp.zeros((CHUNK, 2 * HD), jnp.bfloat16)
        keys[pl.ds(tail, CHUNK), :] = jnp.zeros((CHUNK, HD), jnp.bfloat16)

        def scores_of(queries, at):
            return (
                lax.dot_general(
                    queries, keys[pl.ds(at, CHUNK), :], (((1,), (1,)), ((), ())), preferred_element_type=jnp.float32
                )
                * (SCALE * LOG2E)
            )

        def slab_rows(c, rows):
            queries_at = pl.ds(c * per_group, rows // ROWS)
            end = ends[order[c]] * ROWS
            full = end // CHUNK
            rest = end - full * CHUNK
            total_at = total.at[0:rows, :]

            def plain(i, carry):
                at = pl.multiple_of(i * CHUNK, CHUNK)
                queries = own[queries_at, 0].reshape(rows, HD)
                weights = jnp.exp2(scores_of(queries, at)).astype(jnp.bfloat16)
                total_at[...] += jnp.dot(weights, values[pl.ds(at, CHUNK), :], preferred_element_type=jnp.float32)
                return carry

            def remainder(at):
                queries = own[queries_at, 0].reshape(rows, HD)
                within = lax.broadcasted_iota(jnp.int32, (rows, CHUNK), 1) < rest
                weights = jnp.where(within, jnp.exp2(scores_of(queries, at)), 0.0).astype(jnp.bfloat16)
                total_at[...] += jnp.dot(weights, values[pl.ds(at, CHUNK), :], preferred_element_type=jnp.float32)

            total_at[...] = jnp.zeros((rows, 2 * HD), jnp.float32)
            lax.fori_loop(0, full, plain, 0)

            @pl.when(rest > 0)
            def _():
                remainder(pl.multiple_of(full * CHUNK, CHUNK))

            row = lax.broadcasted_iota(jnp.int32, (rows, HD), 0)
            token = (2 * (row // ROWS) + parity) * ROWS + row % ROWS
            counted = token < valid[c]
            sums = total_at[:, HD : 2 * HD]
            safe = (sums >= LOW) & (sums <= HIGH)
            unsafe = jnp.max(jnp.where(counted & jnp.logical_not(safe), 1.0, 0.0))

            @pl.when(unsafe > 0.0)
            def _():
                peak_at = peak.at[0:rows, :]
                peak_at[...] = jnp.full((rows, HD), -1e30, jnp.float32)
                total_at[...] = jnp.zeros((rows, 2 * HD), jnp.float32)

                def careful(i, carry):
                    at = pl.multiple_of(i * CHUNK, CHUNK)
                    queries = own[queries_at, 0].reshape(rows, HD)
                    within = lax.broadcasted_iota(jnp.int32, (rows, CHUNK), 1) < end - at
                    scores = jnp.where(within, scores_of(queries, at), -1e30)
                    before = peak_at[:, 0:1]
                    now = jnp.maximum(before, jnp.max(scores, axis=1, keepdims=True))
                    weights = jnp.where(within, jnp.exp2(scores - now), 0.0).astype(jnp.bfloat16)
                    total_at[...] = total_at[...] * jnp.exp2(before - now) + jnp.dot(
                        weights, values[pl.ds(at, CHUNK), :], preferred_element_type=jnp.float32
                    )
                    peak_at[...] = jnp.broadcast_to(now, (rows, HD))
                    return carry

                lax.fori_loop(0, (end + CHUNK - 1) // CHUNK, careful, 0)

            result = total_at[:, 0:HD] / total_at[:, HD : 2 * HD]
            result = jnp.where(counted, result, 0.0).astype(jnp.bfloat16)
            out[queries_at] = result.reshape(rows // ROWS, ROWS, HD)
            if rows < slab:
                out[pl.ds(c * per_group + rows // ROWS, (slab - rows) // ROWS)] = jnp.zeros(
                    ((slab - rows) // ROWS, ROWS, HD), jnp.bfloat16
                )

        def visit(c, carry):
            blocks = ((valid[c] + ROWS - 1) // ROWS - parity + 1) // 2
            sizes = (slab // 2, slab * 3 // 4, slab)
            below = 0
            for rows in sizes:
                here = rows // ROWS

                @pl.when((blocks > below) & (blocks <= here))
                def _():
                    slab_rows(c, rows)

                below = here
            return carry

        lax.fori_loop(0, groups, visit, 0)

    @pl.when(active == 0)
    def _():
        out[...] = jnp.zeros_like(out)


def attend(facts, order, valid, own, other):
    slots = own.shape[0]
    groups = order.shape[0]
    tokens = 2 * slots * ROWS
    slab = slots // groups * ROWS
    smem = pl.BlockSpec(memory_space=pltpu.SMEM)
    vmem = pl.BlockSpec(memory_space=pltpu.VMEM)
    return pl.pallas_call(
        functools.partial(attend_kernel, slots),
        out_shape=jax.ShapeDtypeStruct((slots, ROWS, HD), jnp.bfloat16),
        in_specs=[smem, smem, smem, vmem, vmem],
        out_specs=vmem,
        scratch_shapes=[
            pltpu.VMEM((tokens + CHUNK, HD), jnp.bfloat16),
            pltpu.VMEM((tokens + CHUNK, 2 * HD), jnp.bfloat16),
            pltpu.VMEM((slab, 2 * HD), jnp.float32),
            pltpu.VMEM((slab, HD), jnp.float32),
            pltpu.SMEM((groups,), jnp.int32),
            pltpu.SMEM((groups,), jnp.int32),
        ],
        compiler_params=pltpu.CompilerParams(vmem_limit_bytes=40 * 2**20),
    )(facts, order, valid, own, other)


def body(query_rows, key_rows, value_rows, group_order, valid_counts):
    groups, cores = lax.axis_size("group"), lax.axis_size("head")
    devices = groups * cores
    slots = devices // 2
    heads = query_rows.shape[2] // HD
    me = lax.axis_index("group") * cores + lax.axis_index("head")
    same_core = [[i for i in range(devices) if i % 2 == core] for core in range(2)]

    def exchange(x):
        return lax.all_to_all(x, ("group", "head"), 0, 0, axis_index_groups=same_core, tiled=True)

    def by_head(x):
        return x[0].reshape(ROWS, heads, HD).transpose(1, 0, 2)

    packed = jnp.stack([by_head(query_rows), by_head(key_rows), by_head(value_rows)], axis=1)
    packed = jnp.pad(packed, ((0, slots - heads), (0, 0), (0, 0), (0, 0)))
    own = exchange(packed.reshape(slots, 3 * ROWS, HD))
    other = lax.ppermute(own, "head", [(i, i ^ 1) for i in range(cores)])
    facts = jnp.stack([me % 2, (me // 2 < heads).astype(jnp.int32)])
    attended = attend(
        facts,
        group_order,
        valid_counts,
        own.reshape(slots, 3, ROWS, HD),
        other.reshape(slots, 3, ROWS, HD),
    )
    back = exchange(attended)
    return back[:heads].transpose(1, 0, 2).reshape(1, ROWS, heads * HD)


def solution(mesh):
    placed = (
        P("group", "head", None),
        P("group", "head", None),
        P("group", "head", None),
        P(),
        P(),
    )
    return jax.shard_map(
        body, mesh=mesh, in_specs=placed, out_specs=P("group", "head", None), check_vma=False
    )
```

```python
import functools
import math

import jax
import jax.numpy as jnp
from jax import lax
from jax.experimental import pallas as pl
from jax.experimental.pallas import tpu as pltpu
from jax.sharding import PartitionSpec as P

HD = 128
ROWS = 64
TILE = 8
LANES = TILE * ROWS
MAIN = 32
LAST = (8, 16, 24, 32)
SCALE = HD ** (-0.5)
LOG2E = math.log2(math.e)
LOW, HIGH = 1.0, 2.0**110


def attend_kernel(facts, order, valid, own, other, out, packed, queries, total, sums, peak, place, ends, gaps, slot, spot, sems):
    parity, active = facts[0], facts[1]
    groups = order.shape[0]
    per_group = own.shape[0] // groups
    half = per_group // 2

    def blocks_of(j, core):
        return ((valid[j] + ROWS - 1) // ROWS - core + 1) // 2

    def each_copy(p, start, what):
        j = place[p]
        for core in range(2):
            count = blocks_of(j, core)

            def pieces(source, core=core, count=count, start=start):
                def piece(at, size, n):
                    what(
                        pltpu.make_async_copy(
                            source.at[pl.ds(j * per_group + at, size)],
                            packed.at[pl.ds(start + at, size)],
                            sems.at[p, 4 * core + n],
                        )
                    )

                rest = count - half

                @pl.when(rest == half)
                def _():
                    piece(0, per_group, 0)

                @pl.when(rest < half)
                def _():
                    piece(0, half, 1)

                    @pl.when(rest >= 2)
                    def _():
                        piece(half, 2, 2)

                    @pl.when(rest % 2 == 1)
                    def _():
                        piece(half + rest - 1, 1, 3)

            @pl.when(parity == core)
            def _():
                pieces(own)

            @pl.when(parity != core)
            def _():
                pieces(other)

            start = start + count
        return start

    @pl.when(active == 1)
    def _():
        held = jnp.int32(0)
        for j in range(groups):
            place[order[j]] = j
            held = held + blocks_of(j, parity)
        tiles = (held + TILE - 1) // TILE
        pad = tiles * TILE - held

        def begin(p, at):
            start, filled, gap = at
            j = place[p]
            blocks = (valid[j] + ROWS - 1) // ROWS
            ends[p] = start + blocks
            gap = gap + blocks * ROWS - valid[j]
            gaps[p] = gap
            first = start + jnp.where(parity == 0, 0, blocks_of(j, 0))
            for i in range(per_group):
                slot[filled + i] = j * per_group + i
                spot[filled + i] = first + i
            return each_copy(p, start, lambda copy: copy.start()), filled + blocks_of(j, parity), gap

        last, _, _ = lax.fori_loop(0, groups, begin, (jnp.int32(0), pad, jnp.int32(0)))
        packed[pl.ds(last, TILE)] = jnp.zeros((TILE,) + packed.shape[1:], jnp.bfloat16)
        out[...] = jnp.zeros_like(out)

        def arrive(p, start):
            following = each_copy(p, start, lambda copy: copy.wait())
            j = place[p]
            blocks = (valid[j] + ROWS - 1) // ROWS
            block = start + jnp.where(blocks % 2 == 1, blocks_of(j, 0), blocks) - 1
            there = lax.broadcasted_iota(jnp.int32, (ROWS, HD), 0) < valid[j] - (blocks - 1) * ROWS
            for n in (1, 2):
                rows = packed[block, n * ROWS : (n + 1) * ROWS]
                packed[block, n * ROWS : (n + 1) * ROWS] = jnp.where(there, rows, jnp.zeros_like(rows))
            return following

        def scores_of(at, count):
            return (
                lax.dot_general(
                    packed[pl.ds(at, count), ROWS : 2 * ROWS].reshape(count * ROWS, HD),
                    queries[...].reshape(LANES, HD),
                    (((1,), (1,)), ((), ())),
                    preferred_element_type=jnp.float32,
                )
                * (SCALE * LOG2E)
            )

        def mix(at, count, weights):
            return lax.dot_general(
                packed[pl.ds(at, count), 2 * ROWS : 3 * ROWS].reshape(count * ROWS, HD),
                weights.astype(jnp.bfloat16),
                (((0,), (0,)), ((), ())),
                preferred_element_type=jnp.float32,
            )

        def visit(tile, carry):
            here = [slot[tile * TILE + i] for i in range(TILE)]
            ranks = [order[h // per_group] for h in here]
            rows = [valid[h // per_group] - (2 * (h % per_group) + parity) * ROWS for h in here]
            real = [tile * TILE + i >= pad for i in range(TILE)]
            highest = ends[ranks[TILE - 1]]

            needed = jnp.minimum(ranks[TILE - 1] + 2, groups)
            start = lax.fori_loop(carry[0], needed, arrive, carry[1])

            lane = lax.broadcasted_iota(jnp.int32, (1, LANES), 1) // ROWS
            limit = jnp.zeros((1, LANES), jnp.int32)
            rows_left = jnp.zeros((1, LANES), jnp.int32)
            gap = jnp.zeros((1, LANES), jnp.int32)
            for i in range(TILE):
                limit = jnp.where(lane == i, jnp.where(real[i], ends[ranks[i]], 0), limit)
                rows_left = jnp.where(lane == i, jnp.where(real[i], rows[i], 0), rows_left)
                gap = jnp.where(lane == i, gaps[ranks[i]], gap)

                @pl.when(real[i])
                def _():
                    queries[i] = packed[spot[tile * TILE + i], 0:ROWS]

                @pl.when(jnp.logical_not(real[i]))
                def _():
                    queries[i] = jnp.zeros((ROWS, HD), jnp.bfloat16)

            counted = lax.broadcasted_iota(jnp.int32, (1, LANES), 1) % ROWS < rows_left
            total[...] = jnp.zeros_like(total)
            sums[...] = jnp.zeros_like(sums)

            def step(at, count):
                block = lax.broadcasted_iota(jnp.int32, (count, 1, LANES), 0) + at
                bias = jnp.where(block < limit.reshape(1, 1, LANES), 0.0, -1e30)
                scores = scores_of(at, count).reshape(count, ROWS, LANES) + bias
                weights = jnp.exp2(scores).reshape(count * ROWS, LANES)
                sums[...] += jnp.sum(weights.reshape(count * ROWS // 8, 8, LANES), axis=0)
                total[...] += mix(at, count, weights)

            def whole_step(i, c):
                step(i * MAIN, MAIN)
                return c

            full = highest // MAIN
            lax.fori_loop(0, full, whole_step, 0)
            rest = highest - full * MAIN
            below = 0
            for count in LAST:

                @pl.when((rest > below) & (rest <= count))
                def _():
                    step(full * MAIN, count)

                below = count

            whole = jnp.sum(sums[...], axis=0, keepdims=True) - gap.astype(jnp.float32)
            safe = (whole >= LOW) & (whole <= HIGH)
            unsafe = jnp.max(jnp.where(counted & jnp.logical_not(safe), 1.0, 0.0))
            sums[0:1, :] = whole

            @pl.when(unsafe > 0.0)
            def _():
                peak[...] = jnp.full_like(peak, -1e30)
                total[...] = jnp.zeros_like(total)
                sums[...] = jnp.zeros_like(sums)

                def of_group(p, at):
                    j = place[p]
                    for core in range(2):

                        def careful(s, c, at=at, core=core):
                            row = lax.broadcasted_iota(jnp.int32, (ROWS, LANES), 0)
                            within = (row < valid[j] - (2 * s + core) * ROWS) & (at + s < limit)
                            scores = jnp.where(within, scores_of(at + s, 1), -1e30)
                            before = peak[...]
                            now = jnp.maximum(before, jnp.max(scores, axis=0, keepdims=True))
                            shrink = jnp.exp2(before - now)
                            weights = jnp.where(within, jnp.exp2(scores - now), 0.0)
                            sums[0:1, :] = sums[0:1, :] * shrink + jnp.sum(weights, axis=0, keepdims=True)
                            total[...] = total[...] * shrink + mix(at + s, 1, weights)
                            peak[...] = now
                            return c

                        lax.fori_loop(0, blocks_of(j, core), careful, 0)
                        at = at + blocks_of(j, core)
                    return at

                lax.fori_loop(0, ranks[TILE - 1] + 1, of_group, jnp.int32(0))

            result = jnp.where(counted, total[...] / sums[0:1, :], 0.0)
            result = result.T.astype(jnp.bfloat16)
            for i in range(TILE):

                @pl.when(real[i])
                def _():
                    out[here[i]] = result[i * ROWS : (i + 1) * ROWS, :]

            return needed, start

        for i in range(TILE):
            slot[i] = jnp.where(i < pad, slot[pad], slot[i])
        done, start = lax.fori_loop(0, tiles, visit, (jnp.int32(0), jnp.int32(0)))
        lax.fori_loop(done, groups, arrive, start)

    @pl.when(active == 0)
    def _():
        out[...] = jnp.zeros_like(out)


def attend(facts, order, valid, own, other):
    slots = own.shape[0]
    groups = order.shape[0]
    smem = pl.BlockSpec(memory_space=pltpu.SMEM)
    anywhere = pl.BlockSpec(memory_space=pl.ANY)
    per_group = pltpu.SMEM((groups,), jnp.int32)
    listed = pltpu.SMEM((slots + 2 * TILE,), jnp.int32)
    return pl.pallas_call(
        attend_kernel,
        out_shape=jax.ShapeDtypeStruct((slots, ROWS, HD), jnp.bfloat16),
        in_specs=[smem, smem, smem, anywhere, anywhere],
        out_specs=pl.BlockSpec(memory_space=pltpu.VMEM),
        scratch_shapes=[
            pltpu.VMEM((2 * slots + TILE, 3 * ROWS, HD), jnp.bfloat16),
            pltpu.VMEM((TILE, ROWS, HD), jnp.bfloat16),
            pltpu.VMEM((HD, LANES), jnp.float32),
            pltpu.VMEM((8, LANES), jnp.float32),
            pltpu.VMEM((1, LANES), jnp.float32),
            per_group,
            per_group,
            per_group,
            listed,
            listed,
            pltpu.SemaphoreType.DMA((groups, 8)),
        ],
        compiler_params=pltpu.CompilerParams(vmem_limit_bytes=32 * 2**20),
    )(facts, order, valid, own, other)


def body(query_rows, key_rows, value_rows, group_order, valid_counts):
    groups, cores = lax.axis_size("group"), lax.axis_size("head")
    devices = groups * cores
    slots = devices // 2
    heads = query_rows.shape[2] // HD
    me = lax.axis_index("group") * cores + lax.axis_index("head")
    same_core = [[i for i in range(devices) if i % 2 == core] for core in range(2)]

    def exchange(x):
        return lax.all_to_all(x, ("group", "head"), 0, 0, axis_index_groups=same_core, tiled=True)

    def by_head(x):
        return x[0].reshape(ROWS, heads, HD).transpose(1, 0, 2)

    packed = jnp.stack([by_head(query_rows), by_head(key_rows), by_head(value_rows)], axis=1)
    packed = jnp.pad(packed, ((0, slots - heads), (0, 0), (0, 0), (0, 0)))
    own = exchange(packed.reshape(slots, 3 * ROWS, HD))
    other = lax.ppermute(own, "head", [(i, i ^ 1) for i in range(cores)])
    facts = jnp.stack([me % 2, (me // 2 < heads).astype(jnp.int32)])
    attended = attend(
        facts,
        group_order,
        valid_counts,
        own,
        other,
    )
    back = exchange(attended)
    return back[:heads].transpose(1, 0, 2).reshape(1, ROWS, heads * HD)


def solution(mesh):
    placed = (
        P("group", "head", None),
        P("group", "head", None),
        P("group", "head", None),
        P(),
        P(),
    )
    return jax.shard_map(
        body, mesh=mesh, in_specs=placed, out_specs=P("group", "head", None), check_vma=False
    )
```

```python
import functools
import math

import jax
import jax.numpy as jnp
from jax import lax
from jax.experimental import pallas as pl
from jax.experimental.pallas import tpu as pltpu
from jax.sharding import PartitionSpec as P

HD = 128
ROWS = 64
TILE = 8
LANES = TILE * ROWS
MAIN = 32
LAST = (8, 16, 24, 32)
SCALE = HD ** (-0.5)
LOG2E = math.log2(math.e)
LOW, HIGH = 1.0, 2.0**110


def attend_kernel(facts, order, valid, own, other, out, keys, values, queries, total, sums, peak, unsafe, place, starts, gaps, slot):
    parity, active = facts[0], facts[1]
    groups = order.shape[0]
    per_group = own.shape[0] // groups

    def blocks_of(j, core):
        return ((valid[j] + ROWS - 1) // ROWS - core + 1) // 2

    @pl.when(active == 1)
    def _():
        held = jnp.int32(0)
        for j in range(groups):
            place[order[j]] = j
            held = held + blocks_of(j, parity)
        tiles = (held + TILE - 1) // TILE
        pad = tiles * TILE - held
        start, filled, gap = jnp.int32(0), pad, jnp.int32(0)
        for p in range(groups):
            j = place[p]
            blocks = (valid[j] + ROWS - 1) // ROWS
            starts[p] = start
            start = start + blocks
            gap = gap + blocks * ROWS - valid[j]
            gaps[p] = gap
            for i in range(per_group):
                slot[filled + i] = j * per_group + i
            filled = filled + blocks_of(j, parity)
        starts[groups] = start
        for i in range(TILE):
            slot[i] = jnp.where(i < pad, slot[pad], slot[i])
        out[...] = jnp.zeros_like(out)
        unsafe[...] = jnp.zeros_like(unsafe)

        def arrive(p, carry):
            j = place[p]
            for core in range(2):
                at = starts[p] + (blocks_of(j, 0) if core == 1 else 0)

                def take(source, at=at):
                    slab = source[pl.ds(j * per_group, per_group)]
                    keys[pl.ds(at, per_group)] = slab[:, ROWS : 2 * ROWS]
                    values[pl.ds(at, per_group)] = slab[:, 2 * ROWS : 3 * ROWS]

                @pl.when(parity == core)
                def _():
                    take(own)

                @pl.when(parity != core)
                def _():
                    take(other)

            blocks = (valid[j] + ROWS - 1) // ROWS
            block = starts[p] + jnp.where(blocks % 2 == 1, blocks_of(j, 0), blocks) - 1
            there = lax.broadcasted_iota(jnp.int32, (ROWS, HD), 0) < valid[j] - (blocks - 1) * ROWS
            for ref in (keys, values):
                rows = ref[block]
                ref[block] = jnp.where(there, rows, jnp.zeros_like(rows))

            @pl.when(p == groups - 1)
            def _():
                values[pl.ds(starts[groups], TILE)] = jnp.zeros((TILE, ROWS, HD), jnp.bfloat16)

            return carry

        def scores_of(at, count):
            return (
                lax.dot_general(
                    keys[pl.ds(at, count)].reshape(count * ROWS, HD),
                    queries[...].reshape(LANES, HD),
                    (((1,), (1,)), ((), ())),
                    preferred_element_type=jnp.float32,
                )
                * (SCALE * LOG2E)
            )

        def mix(at, count, weights):
            return lax.dot_general(
                values[pl.ds(at, count)].reshape(count * ROWS, HD),
                weights.astype(jnp.bfloat16),
                (((0,), (0,)), ((), ())),
                preferred_element_type=jnp.float32,
            )

        def tile_of(tile):
            lane = lax.broadcasted_iota(jnp.int32, (1, LANES), 1) // ROWS
            limit = jnp.zeros((1, LANES), jnp.int32)
            rows_left = jnp.zeros((1, LANES), jnp.int32)
            gap = jnp.zeros((1, LANES), jnp.int32)
            lowest = jnp.int32(0)
            for i in range(TILE):
                here = slot[tile * TILE + i]
                j = here // per_group
                rank = order[j]
                end = starts[rank + 1]
                real = tile * TILE + i >= pad
                rows = jnp.where(real, valid[j] - (2 * (here % per_group) + parity) * ROWS, 0)
                limit = jnp.where(lane == i, end, limit)
                rows_left = jnp.where(lane == i, rows, rows_left)
                gap = jnp.where(lane == i, gaps[rank], gap)
                queries[i] = own[here, 0:ROWS]
                lowest = end if i == 0 else lowest
            counted = lax.broadcasted_iota(jnp.int32, (1, LANES), 1) % ROWS < rows_left
            return limit, counted, gap, lowest, end, rank

        def finish(tile, counted):
            result = jnp.where(counted, total[...] * (1.0 / sums[0:1, :]), 0.0)
            result = result.T.astype(jnp.bfloat16)
            for i in range(TILE):

                @pl.when(tile * TILE + i >= pad)
                def _():
                    out[slot[tile * TILE + i]] = result[i * ROWS : (i + 1) * ROWS, :]

        def visit(tile, arrived):
            limit, counted, gap, lowest, highest, rank = tile_of(tile)
            needed = jnp.minimum(rank + 2, groups)
            lax.fori_loop(arrived, needed, arrive, 0)
            total[...] = jnp.zeros_like(total)
            sums[...] = jnp.zeros_like(sums)

            def step(at, count, masked):
                scores = scores_of(at, count)
                if masked:
                    block = lax.broadcasted_iota(jnp.int32, (count, 1, LANES), 0) + at
                    bias = jnp.where(block < limit.reshape(1, 1, LANES), 0.0, -1e30)
                    scores = (scores.reshape(count, ROWS, LANES) + bias).reshape(count * ROWS, LANES)
                weights = jnp.exp2(scores)
                sums[...] += jnp.sum(weights.reshape(count * ROWS // 8, 8, LANES), axis=0)
                total[...] += mix(at, count, weights)

            def plain(i, c):
                step(i * MAIN, MAIN, False)
                return c

            def masked(i, c):
                step(i * MAIN, MAIN, True)
                return c

            open_steps = lowest // MAIN
            steps = highest // MAIN
            lax.fori_loop(0, open_steps, plain, 0)
            lax.fori_loop(open_steps, steps, masked, 0)
            rest = highest - steps * MAIN
            below = 0
            for count in LAST:

                @pl.when((rest > below) & (rest <= count))
                def _():
                    step(steps * MAIN, count, True)

                below = count

            whole = jnp.sum(sums[...], axis=0, keepdims=True) - gap.astype(jnp.float32)
            safe = (whole >= LOW) & (whole <= HIGH)
            unsafe[...] = jnp.maximum(unsafe[...], jnp.where(counted & jnp.logical_not(safe), 1.0, 0.0))
            sums[0:1, :] = whole
            finish(tile, counted)
            return needed

        lax.fori_loop(0, tiles, visit, jnp.int32(0))

        @pl.when(jnp.max(unsafe[...]) > 0.0)
        def _():
            def again(tile, carry):
                limit, counted, _, _, _, rank = tile_of(tile)
                peak[...] = jnp.full_like(peak, -1e30)
                total[...] = jnp.zeros_like(total)
                sums[...] = jnp.zeros_like(sums)

                def of_group(p, c):
                    j = place[p]
                    for core in range(2):
                        at = starts[p] + (blocks_of(j, 0) if core == 1 else 0)

                        def careful(s, c, at=at, core=core):
                            row = lax.broadcasted_iota(jnp.int32, (ROWS, LANES), 0)
                            within = (row < valid[j] - (2 * s + core) * ROWS) & (at + s < limit)
                            scores = jnp.where(within, scores_of(at + s, 1), -1e30)
                            before = peak[...]
                            now = jnp.maximum(before, jnp.max(scores, axis=0, keepdims=True))
                            shrink = jnp.exp2(before - now)
                            weights = jnp.where(within, jnp.exp2(scores - now), 0.0)
                            sums[0:1, :] = sums[0:1, :] * shrink + jnp.sum(weights, axis=0, keepdims=True)
                            total[...] = total[...] * shrink + mix(at + s, 1, weights)
                            peak[...] = now
                            return c

                        lax.fori_loop(0, blocks_of(j, core), careful, 0)
                    return c

                lax.fori_loop(0, rank + 1, of_group, 0)
                finish(tile, counted)
                return carry

            lax.fori_loop(0, tiles, again, 0)

    @pl.when(active == 0)
    def _():
        out[...] = jnp.zeros_like(out)


def attend(facts, order, valid, own, other):
    slots = own.shape[0]
    groups = order.shape[0]
    smem = pl.BlockSpec(memory_space=pltpu.SMEM)
    vmem = pl.BlockSpec(memory_space=pltpu.VMEM)
    packed = pltpu.VMEM((2 * slots + TILE, ROWS, HD), jnp.bfloat16)
    per_group = pltpu.SMEM((groups + 1,), jnp.int32)
    return pl.pallas_call(
        attend_kernel,
        out_shape=jax.ShapeDtypeStruct((slots, ROWS, HD), jnp.bfloat16),
        in_specs=[smem, smem, smem, vmem, vmem],
        out_specs=vmem,
        scratch_shapes=[
            packed,
            packed,
            pltpu.VMEM((TILE, ROWS, HD), jnp.bfloat16),
            pltpu.VMEM((HD, LANES), jnp.float32),
            pltpu.VMEM((8, LANES), jnp.float32),
            pltpu.VMEM((1, LANES), jnp.float32),
            pltpu.VMEM((1, LANES), jnp.float32),
            per_group,
            per_group,
            per_group,
            pltpu.SMEM((slots + 2 * TILE,), jnp.int32),
        ],
        compiler_params=pltpu.CompilerParams(vmem_limit_bytes=24 * 2**20),
    )(facts, order, valid, own, other)


def split_kernel(heads, query_rows, key_rows, value_rows, out, sem):
    for h in range(heads):
        for n, rows in enumerate((query_rows, key_rows, value_rows)):
            pltpu.make_async_copy(
                rows.at[0, :, h * HD : (h + 1) * HD], out.at[h, n * ROWS : (n + 1) * ROWS], sem
            ).start()
    everything = out.at[0:heads]
    pltpu.make_async_copy(everything, everything, sem).wait()


def split_heads(slots, query_rows, key_rows, value_rows):
    hbm = pl.BlockSpec(memory_space=pltpu.HBM)
    return pl.pallas_call(
        functools.partial(split_kernel, query_rows.shape[2] // HD),
        out_shape=jax.ShapeDtypeStruct((slots, 3 * ROWS, HD), query_rows.dtype),
        in_specs=[hbm] * 3,
        out_specs=pl.BlockSpec(memory_space=pltpu.VMEM),
        scratch_shapes=[pltpu.SemaphoreType.DMA],
        compiler_params=pltpu.CompilerParams(vmem_limit_bytes=8 * 2**20),
    )(query_rows, key_rows, value_rows)


def join_kernel(heads, attended, out, sem):
    for h in range(heads):
        pltpu.make_async_copy(attended.at[h], out.at[0, :, h * HD : (h + 1) * HD], sem).start()
    pltpu.make_async_copy(out, out, sem).wait()


def join_heads(heads, attended):
    return pl.pallas_call(
        functools.partial(join_kernel, heads),
        out_shape=jax.ShapeDtypeStruct((1, ROWS, heads * HD), attended.dtype),
        in_specs=[pl.BlockSpec(memory_space=pltpu.VMEM)],
        out_specs=pl.BlockSpec(memory_space=pltpu.HBM),
        scratch_shapes=[pltpu.SemaphoreType.DMA],
        compiler_params=pltpu.CompilerParams(vmem_limit_bytes=8 * 2**20),
    )(attended)


def body(query_rows, key_rows, value_rows, group_order, valid_counts):
    groups, cores = lax.axis_size("group"), lax.axis_size("head")
    devices = groups * cores
    slots = devices // 2
    heads = query_rows.shape[2] // HD
    me = lax.axis_index("group") * cores + lax.axis_index("head")
    same_core = [[i for i in range(devices) if i % 2 == core] for core in range(2)]

    def exchange(x):
        return lax.all_to_all(x, ("group", "head"), 0, 0, axis_index_groups=same_core, tiled=True)

    own = exchange(split_heads(slots, query_rows, key_rows, value_rows))
    other = lax.ppermute(own, "head", [(i, i ^ 1) for i in range(cores)])
    facts = jnp.stack([me % 2, (me // 2 < heads).astype(jnp.int32)])
    attended = attend(
        facts,
        group_order,
        valid_counts,
        own,
        other,
    )
    return join_heads(heads, exchange(attended))


def solution(mesh):
    placed = (
        P("group", "head", None),
        P("group", "head", None),
        P("group", "head", None),
        P(),
        P(),
    )
    return jax.shard_map(
        body, mesh=mesh, in_specs=placed, out_specs=P("group", "head", None), check_vma=False
    )
```

```python
import functools
import math

import jax
import jax.numpy as jnp
from jax import lax
from jax.experimental import pallas as pl
from jax.experimental.pallas import tpu as pltpu
from jax.sharding import PartitionSpec as P

HD = 128
ROWS = 64
TILE = 8
LANES = TILE * ROWS
MAIN = 64
LAST = (8, 16, 24, 32, 40, 48, 56, 64)
SHIFT = ROWS.bit_length() - 1
PLACE, TILES, PAD, PARITY, ACTIVE, STARTS = 0, 8, 9, 10, 11, (16, 32)
SLOT, LEFT, RANK, END, GAP = 48, 128, 208, (288, 368), (448, 528)
SIZE = 608
SCALE = HD ** (-0.5)
LOG2E = math.log2(math.e)
LOW, HIGH = 1.0, 2.0**110


def attend_kernel(first, *refs):
    if first:
        table, valid, lanes, own, total_out, sums_out, *scratch = refs
        keys, values, queries = scratch
    else:
        table, valid, lanes, own, other, total_in, sums_in, out, *scratch = refs
        keys, values, queries, landed, total, sums, peak, unsafe, sems = scratch
    parity, active = table[PARITY], table[ACTIVE]
    which = 0 if first else 1
    core = parity if first else 1 - parity
    groups = valid.shape[0]
    per_group = own.shape[0] // groups

    def all_blocks(j):
        return jnp.right_shift(valid[j] + ROWS - 1, SHIFT)

    def landing(p):
        return pltpu.make_async_copy(
            other.at[pl.ds(table[PLACE + p] * per_group, per_group), pl.ds(ROWS, 2 * ROWS)],
            landed.at[pl.ds(p * per_group, per_group)],
            sems.at[p],
        )

    @pl.when(active == 1)
    def _():
        if not first:
            for p in range(groups):
                landing(p).start()
            out[...] = jnp.zeros_like(out)
            unsafe[...] = jnp.zeros_like(unsafe)
        tiles, pad = table[TILES], table[PAD]

        def arrive(p, carry):
            j = table[PLACE + p]
            at = table[STARTS[which] + p]
            if first:
                slab = own[pl.ds(j * per_group, per_group), ROWS : 3 * ROWS]
            else:
                landing(p).wait()
                slab = landed[pl.ds(p * per_group, per_group)]
            keys[pl.ds(at, per_group)] = slab[:, 0:ROWS]
            values[pl.ds(at, per_group)] = slab[:, ROWS : 2 * ROWS]
            blocks = all_blocks(j)

            @pl.when(jnp.bitwise_and(blocks - 1, 1) == core)
            def _():
                block = table[STARTS[which] + p + 1] - 1
                there = lax.broadcasted_iota(jnp.int32, (ROWS, HD), 0) < valid[j] - (blocks - 1) * ROWS
                for ref in (keys, values):
                    rows = ref[block]
                    ref[block] = jnp.where(there, rows, jnp.zeros_like(rows))

            @pl.when(p == groups - 1)
            def _():
                values[pl.ds(table[STARTS[which] + groups], TILE)] = jnp.zeros((TILE, ROWS, HD), jnp.bfloat16)

            return carry

        def scores_of(rows):
            return (
                lax.dot_general(
                    rows,
                    queries[...].reshape(LANES, HD),
                    (((1,), (1,)), ((), ())),
                    preferred_element_type=jnp.float32,
                )
                * (SCALE * LOG2E)
            )

        def mix(rows, weights):
            return lax.dot_general(
                rows,
                weights.astype(jnp.bfloat16),
                (((0,), (0,)), ((), ())),
                preferred_element_type=jnp.float32,
            )

        def take_queries(tile):
            for i in range(TILE):
                queries[i] = own[table[SLOT + tile * TILE + i], 0:ROWS]

        def counted_of(tile):
            row = jnp.bitwise_and(lax.broadcasted_iota(jnp.int32, (1, LANES), 1), ROWS - 1)
            return row < lanes[tile, 4:5, :]

        def finish(tile, counted):
            result = jnp.where(counted, total[...] * (1.0 / sums[0:1, :]), 0.0)
            result = result.astype(jnp.bfloat16).T
            for i in range(TILE):

                @pl.when(tile * TILE + i >= pad)
                def _():
                    out[table[SLOT + tile * TILE + i]] = result[i * ROWS : (i + 1) * ROWS, :]

        def visit(tile, arrived):
            take_queries(tile)
            limit = lanes[tile, which : which + 1, :]
            gap = lanes[tile, 2 + which : 3 + which, :]
            lowest = table[END[which] + tile * TILE]
            highest = table[END[which] + tile * TILE + TILE - 1]
            rank = table[RANK + tile * TILE + TILE - 1]
            needed = jnp.minimum(rank + 3, groups)
            lax.fori_loop(arrived, needed, arrive, 0)
            if first:
                total_at, sums_at = total_out.at[tile], sums_out.at[tile]
                total_at[...] = jnp.zeros((HD, LANES), jnp.float32)
                lead = lax.broadcasted_iota(jnp.int32, (8, LANES), 0) == 0
                sums_at[...] = jnp.where(lead, -gap.astype(jnp.float32), 0.0)
            else:
                total_at, sums_at = total, sums
                total[...] = total_in[tile]
                lead = lax.broadcasted_iota(jnp.int32, (8, LANES), 0) == 0
                sums[...] = sums_in[tile] - jnp.where(lead, gap.astype(jnp.float32), 0.0)

            def step(at, count, masked):
                scores = scores_of(keys[pl.ds(at, count)].reshape(count * ROWS, HD))
                if masked:
                    block = lax.broadcasted_iota(jnp.int32, (count, 1, LANES), 0) + at
                    bias = jnp.where(block < limit.reshape(1, 1, LANES), 0.0, -1e30)
                    scores = (scores.reshape(count, ROWS, LANES) + bias).reshape(count * ROWS, LANES)
                weights = jnp.exp2(scores)
                sums_at[...] += jnp.sum(weights.reshape(count * ROWS // 8, 8, LANES), axis=0)
                total_at[...] += mix(values[pl.ds(at, count)].reshape(count * ROWS, HD), weights)

            def plain(i, c):
                step(i * MAIN, MAIN, False)
                return c

            def masked(i, c):
                step(i * MAIN, MAIN, True)
                return c

            open_steps = jnp.right_shift(lowest, MAIN.bit_length() - 1)
            steps = jnp.right_shift(highest, MAIN.bit_length() - 1)
            lax.fori_loop(0, open_steps, plain, 0)
            lax.fori_loop(open_steps, steps, masked, 0)
            rest = highest - steps * MAIN
            below = 0
            for count in LAST:

                @pl.when((rest > below) & (rest <= count))
                def _():
                    step(steps * MAIN, count, True)

                below = count

            if not first:
                counted = counted_of(tile)
                whole = jnp.sum(sums[...], axis=0, keepdims=True)
                safe = (whole >= LOW) & (whole <= HIGH)
                unsafe[...] = jnp.maximum(unsafe[...], jnp.where(counted & jnp.logical_not(safe), 1.0, 0.0))
                sums[0:1, :] = whole
                finish(tile, counted)
            return needed

        arrived = lax.fori_loop(0, tiles, visit, jnp.int32(0))
        if first:
            return
        lax.fori_loop(arrived, groups, arrive, 0)

        @pl.when(jnp.max(unsafe[...]) > 0.0)
        def _():
            def again(tile, carry):
                take_queries(tile)
                counted = counted_of(tile)
                ranks = lanes[tile, 5:6, :]
                rank = table[RANK + tile * TILE + TILE - 1]
                peak[...] = jnp.full_like(peak, -1e30)
                total[...] = jnp.zeros_like(total)
                sums[...] = jnp.zeros_like(sums)

                def of_group(p, c):
                    j = table[PLACE + p]
                    for side in range(2):

                        def careful(s, c, side=side):
                            block = jnp.where(
                                parity == side,
                                own[j * per_group + s, ROWS : 3 * ROWS],
                                landed[p * per_group + s],
                            )
                            row = lax.broadcasted_iota(jnp.int32, (ROWS, LANES), 0)
                            within = (row < valid[j] - (2 * s + side) * ROWS) & (p <= ranks)
                            scores = jnp.where(within, scores_of(block[0:ROWS]), -1e30)
                            before = peak[...]
                            now = jnp.maximum(before, jnp.max(scores, axis=0, keepdims=True))
                            shrink = jnp.exp2(before - now)
                            weights = jnp.where(within, jnp.exp2(scores - now), 0.0)
                            sums[0:1, :] = sums[0:1, :] * shrink + jnp.sum(weights, axis=0, keepdims=True)
                            total[...] = total[...] * shrink + mix(block[ROWS : 2 * ROWS], weights)
                            peak[...] = now
                            return c

                        lax.fori_loop(0, jnp.right_shift(all_blocks(j) + 1 - side, 1), careful, 0)
                    return c

                lax.fori_loop(0, rank + 1, of_group, 0)
                finish(tile, counted)
                return carry

            lax.fori_loop(0, tiles, again, 0)

    if not first:

        @pl.when(active == 0)
        def _():
            out[...] = jnp.zeros_like(out)


def attend_call(table, valid, lanes, own, other, state):
    first = other is None
    slots = own.shape[0]
    groups = valid.shape[0]
    smem = pl.BlockSpec(memory_space=pltpu.SMEM)
    vmem = pl.BlockSpec(memory_space=pltpu.VMEM)
    hbm = pl.BlockSpec(memory_space=pltpu.HBM)
    packed = pltpu.VMEM((slots + TILE, ROWS, HD), jnp.bfloat16)
    scratch = [packed, packed, pltpu.VMEM((TILE, ROWS, HD), jnp.bfloat16)]
    work = slots * ROWS * slots * ROWS // 2
    if first:
        tiles = slots // TILE
        operands, specs = (own,), [vmem]
        shapes = (
            jax.ShapeDtypeStruct((tiles, HD, LANES), jnp.float32),
            jax.ShapeDtypeStruct((tiles, 8, LANES), jnp.float32),
        )
        out_specs = (vmem, vmem)
    else:
        operands, specs = (own, other, *state), [vmem, hbm, vmem, vmem]
        shapes = jax.ShapeDtypeStruct((slots, ROWS, HD), jnp.bfloat16)
        out_specs = vmem
        scratch += [
            pltpu.VMEM((slots, 2 * ROWS, HD), jnp.bfloat16),
            pltpu.VMEM((HD, LANES), jnp.float32),
            pltpu.VMEM((8, LANES), jnp.float32),
            pltpu.VMEM((1, LANES), jnp.float32),
            pltpu.VMEM((1, LANES), jnp.float32),
            pltpu.SemaphoreType.DMA((groups,)),
        ]
    return pl.pallas_call(
        functools.partial(attend_kernel, first),
        out_shape=shapes,
        in_specs=[smem, smem, vmem, *specs],
        out_specs=out_specs,
        scratch_shapes=scratch,
        compiler_params=pltpu.CompilerParams(vmem_limit_bytes=36 * 2**20),
        cost_estimate=pl.CostEstimate(flops=4 * HD * work, bytes_accessed=8 * 2**20, transcendentals=work),
    )(table, valid, lanes, *operands)


def attend(table, valid, lanes, own, other):
    state = attend_call(table, valid, lanes, own, None, ())
    return attend_call(table, valid, lanes, own, other, state)


def plan(order, valid, parity, per_group, table):
    groups = order.shape[0]
    for j in range(groups):
        table[PLACE + order[j]] = j
    starts = [jnp.int32(0), jnp.int32(0)]
    gaps = [jnp.int32(0), jnp.int32(0)]
    held = jnp.int32(0)
    for j in range(groups):
        held = held + jnp.right_shift(jnp.right_shift(valid[j] + ROWS - 1, SHIFT) + 1 - parity, 1)
    tiles = jnp.right_shift(held + TILE - 1, TILE.bit_length() - 1)
    pad = tiles * TILE - held
    table[TILES], table[PAD] = tiles, pad
    filled = pad
    for p in range(groups):
        j = table[PLACE + p]
        blocks = jnp.right_shift(valid[j] + ROWS - 1, SHIFT)
        gap = blocks * ROWS - valid[j]
        last_core = jnp.bitwise_and(blocks - 1, 1)
        counts = [jnp.right_shift(blocks + 1 - core, 1) for core in (parity, 1 - parity)]
        for which, core in enumerate((parity, 1 - parity)):
            table[STARTS[which] + p] = starts[which]
            starts[which] = starts[which] + counts[which]
            gaps[which] = gaps[which] + jnp.where(last_core == core, gap, 0)
        for i in range(per_group):
            at = filled + i
            table[SLOT + at] = j * per_group + i
            table[LEFT + at] = valid[j] - (2 * i + parity) * ROWS
            table[RANK + at] = p
            for which in range(2):
                table[END[which] + at] = starts[which]
                table[GAP[which] + at] = gaps[which]
        filled = filled + counts[0]
    for which in range(2):
        table[STARTS[which] + groups] = starts[which]
    for i in range(TILE):
        front = i < pad
        table[SLOT + i] = jnp.where(front, table[SLOT + pad], table[SLOT + i])
        table[LEFT + i] = jnp.where(front, 0, table[LEFT + i])
        table[RANK + i] = jnp.where(front, table[RANK + pad], table[RANK + i])
        for base in (*END, *GAP):
            table[base + i] = jnp.where(front, table[base + pad], table[base + i])


def describe_tiles(table, lanes):
    def describe(tile, carry):
        for i in range(TILE):
            for n, base in enumerate((END[0], END[1], GAP[0], GAP[1], LEFT, RANK)):
                of_block = jnp.full((1, ROWS), table[base + tile * TILE + i], jnp.int32)
                lanes[tile, n : n + 1, i * ROWS : (i + 1) * ROWS] = of_block
        return carry

    lax.fori_loop(0, table[TILES], describe, 0)


def split_kernel(heads, order, valid, query_rows, key_rows, value_rows, out, table, lanes, staged, taken, given):
    inputs = (query_rows, key_rows, value_rows)
    arrivals = [pltpu.make_async_copy(rows.at[0], staged.at[n], taken.at[n]) for n, rows in enumerate(inputs)]
    for copy in arrivals:
        copy.start()
    parity = jnp.bitwise_and(lax.axis_index("head"), 1)
    chip = (lax.axis_index("group") * lax.axis_size("head") + lax.axis_index("head") - parity) // 2
    table[PARITY], table[ACTIVE] = parity, (chip < heads).astype(jnp.int32)
    plan(order, valid, parity, lanes.shape[0] * TILE // order.shape[0], table)
    for n, copy in enumerate(arrivals):
        copy.wait()
        for h in range(heads):
            pltpu.make_async_copy(
                staged.at[n, :, h * HD : (h + 1) * HD], out.at[h, n * ROWS : (n + 1) * ROWS], given
            ).start()
    describe_tiles(table, lanes)
    everything = out.at[0:heads]
    pltpu.make_async_copy(everything, everything, given).wait()


def split_heads(slots, order, valid, query_rows, key_rows, value_rows):
    smem = pl.BlockSpec(memory_space=pltpu.SMEM)
    hbm = pl.BlockSpec(memory_space=pltpu.HBM)
    return pl.pallas_call(
        functools.partial(split_kernel, query_rows.shape[2] // HD),
        out_shape=(
            jax.ShapeDtypeStruct((slots, 3 * ROWS, HD), query_rows.dtype),
            jax.ShapeDtypeStruct((SIZE,), jnp.int32),
            jax.ShapeDtypeStruct((slots // TILE, 8, LANES), jnp.int32),
        ),
        in_specs=[smem, smem, hbm, hbm, hbm],
        out_specs=(hbm, smem, pl.BlockSpec(memory_space=pltpu.VMEM)),
        scratch_shapes=[
            pltpu.VMEM((3, *query_rows.shape[1:]), query_rows.dtype),
            pltpu.SemaphoreType.DMA((3,)),
            pltpu.SemaphoreType.DMA,
        ],
        compiler_params=pltpu.CompilerParams(vmem_limit_bytes=61 * 2**20),
    )(order, valid, query_rows, key_rows, value_rows)


def join_kernel(heads, attended, out, sem):
    for h in range(heads):
        pltpu.make_async_copy(attended.at[h], out.at[0, :, h * HD : (h + 1) * HD], sem).start()
    pltpu.make_async_copy(out, out, sem).wait()


def join_heads(heads, attended):
    return pl.pallas_call(
        functools.partial(join_kernel, heads),
        out_shape=jax.ShapeDtypeStruct((1, ROWS, heads * HD), attended.dtype),
        in_specs=[pl.BlockSpec(memory_space=pltpu.VMEM)],
        out_specs=pl.BlockSpec(memory_space=pltpu.HBM),
        scratch_shapes=[pltpu.SemaphoreType.DMA],
        compiler_params=pltpu.CompilerParams(vmem_limit_bytes=8 * 2**20),
    )(attended)


def body(query_rows, key_rows, value_rows, group_order, valid_counts):
    groups, cores = lax.axis_size("group"), lax.axis_size("head")
    devices = groups * cores
    slots = devices // 2
    heads = query_rows.shape[2] // HD
    same_core = [[i for i in range(devices) if i % 2 == core] for core in range(2)]

    def exchange(x):
        return lax.all_to_all(x, ("group", "head"), 0, 0, axis_index_groups=same_core, tiled=True)

    sent, table, lanes = split_heads(slots, group_order, valid_counts, query_rows, key_rows, value_rows)
    own = exchange(sent)
    other = lax.ppermute(own, "head", [(i, i ^ 1) for i in range(cores)])
    attended = attend(table, valid_counts, lanes, own, other)
    return join_heads(heads, exchange(attended))


def solution(mesh):
    placed = (
        P("group", "head", None),
        P("group", "head", None),
        P("group", "head", None),
        P(),
        P(),
    )
    return jax.shard_map(
        body, mesh=mesh, in_specs=placed, out_specs=P("group", "head", None), check_vma=False
    )
```

```python
import functools
import math

import jax
import jax.numpy as jnp
from jax import lax
from jax.experimental import pallas as pl
from jax.experimental.pallas import tpu as pltpu
from jax.sharding import PartitionSpec as P

HD = 128
ROWS = 64
TILE = 8
LANES = TILE * ROWS
MAIN = 64
LAST = (8, 16, 24, 32, 40, 48, 56, 64)
SHIFT = ROWS.bit_length() - 1
PLACE, TILES, PAD, PARITY, ACTIVE, STARTS = 0, 8, 9, 10, 11, (16, 32)
SLOT, LEFT, RANK, END, GAP = 48, 128, 208, (288, 368), (448, 528)
SIZE = 608
EDGE = 24
SCALE = HD ** (-0.5)
LOG2E = math.log2(math.e)
LOW, HIGH = 1.0, 2.0**110


def attend_kernel(first, *refs):
    if first:
        table, valid, lanes, own, total_out, sums_out, *scratch = refs
        keys, values, queries = scratch
    else:
        table, valid, lanes, own, other, total_in, sums_in, out, *scratch = refs
        keys, values, queries, landed, total, sums, peak, unsafe, sems = scratch
    parity, active = table[PARITY], table[ACTIVE]
    which = 0 if first else 1
    core = parity if first else 1 - parity
    groups = valid.shape[0]
    per_group = own.shape[0] // groups

    def all_blocks(j):
        return jnp.right_shift(valid[j] + ROWS - 1, SHIFT)

    def landing(p):
        return pltpu.make_async_copy(
            other.at[pl.ds(table[PLACE + p] * per_group, per_group), pl.ds(ROWS, 2 * ROWS)],
            landed.at[pl.ds(p * per_group, per_group)],
            sems.at[p],
        )

    @pl.when(active == 1)
    def _():
        if not first:
            for p in range(groups):
                landing(p).start()
            out[...] = jnp.zeros_like(out)
            unsafe[...] = jnp.zeros_like(unsafe)
        tiles, pad = table[TILES], table[PAD]

        def arrive(p, carry):
            j = table[PLACE + p]
            at = table[STARTS[which] + p]
            if first:
                slab = own[pl.ds(j * per_group, per_group), ROWS : 3 * ROWS]
            else:
                landing(p).wait()
                slab = landed[pl.ds(p * per_group, per_group)]
            keys[pl.ds(at, per_group)] = slab[:, 0:ROWS]
            values[pl.ds(at, per_group)] = slab[:, ROWS : 2 * ROWS]
            blocks = all_blocks(j)

            @pl.when(jnp.bitwise_and(blocks - 1, 1) == core)
            def _():
                block = table[STARTS[which] + p + 1] - 1
                there = lax.broadcasted_iota(jnp.int32, (ROWS, HD), 0) < valid[j] - (blocks - 1) * ROWS
                for ref in (keys, values):
                    rows = ref[block]
                    ref[block] = jnp.where(there, rows, jnp.zeros_like(rows))

            @pl.when(p == groups - 1)
            def _():
                values[pl.ds(table[STARTS[which] + groups], TILE)] = jnp.zeros((TILE, ROWS, HD), jnp.bfloat16)

            return carry

        def scores_of(rows):
            return (
                lax.dot_general(
                    rows,
                    queries[...].reshape(LANES, HD),
                    (((1,), (1,)), ((), ())),
                    preferred_element_type=jnp.float32,
                )
                * (SCALE * LOG2E)
            )

        def mix(rows, weights):
            return lax.dot_general(
                rows,
                weights.astype(jnp.bfloat16),
                (((0,), (0,)), ((), ())),
                preferred_element_type=jnp.float32,
            )

        def take_queries(tile):
            for i in range(TILE):
                queries[i] = own[table[SLOT + tile * TILE + i], 0:ROWS]

        def counted_of(tile):
            row = jnp.bitwise_and(lax.broadcasted_iota(jnp.int32, (1, LANES), 1), ROWS - 1)
            return row < lanes[tile, 4:5, :]

        def finish(tile, counted):
            result = jnp.where(counted, total[...] * (1.0 / sums[0:1, :]), 0.0)
            result = result.astype(jnp.bfloat16).T
            for i in range(TILE):

                @pl.when(tile * TILE + i >= pad)
                def _():
                    out[table[SLOT + tile * TILE + i]] = result[i * ROWS : (i + 1) * ROWS, :]

        def visit(tile, arrived):
            take_queries(tile)
            limit = lanes[tile, which : which + 1, :]
            gap = lanes[tile, 2 + which : 3 + which, :]
            lowest = table[END[which] + tile * TILE]
            highest = table[END[which] + tile * TILE + TILE - 1]
            rank = table[RANK + tile * TILE + TILE - 1]
            needed = jnp.minimum(rank + 3, groups)
            lax.fori_loop(arrived, needed, arrive, 0)
            if first:
                total_at, sums_at = total_out.at[tile], sums_out.at[tile]
                total_at[...] = jnp.zeros((HD, LANES), jnp.float32)
                lead = lax.broadcasted_iota(jnp.int32, (8, LANES), 0) == 0
                sums_at[...] = jnp.where(lead, -gap.astype(jnp.float32), 0.0)
            else:
                total_at, sums_at = total, sums
                total[...] = total_in[tile]
                lead = lax.broadcasted_iota(jnp.int32, (8, LANES), 0) == 0
                sums[...] = sums_in[tile] - jnp.where(lead, gap.astype(jnp.float32), 0.0)

            def step(at, count, masked, final=False):
                scores = scores_of(keys[pl.ds(at, count)].reshape(count * ROWS, HD))
                open_rows = 0
                if masked:
                    edge = count if count == MAIN and not final else min(count, EDGE)
                    open_rows = (count - edge) * ROWS
                    block = lax.broadcasted_iota(jnp.int32, (edge, 1, LANES), 0) + (at + count - edge)
                    bias = jnp.where(block < limit.reshape(1, 1, LANES), 0.0, -1e30)
                    shut = (scores[open_rows:].reshape(edge, ROWS, LANES) + bias).reshape(edge * ROWS, LANES)
                    scores = jnp.concatenate([scores[:open_rows], shut], axis=0) if open_rows else shut
                weights = jnp.exp2(scores)
                sums_at[...] += jnp.sum(weights.reshape(count * ROWS // 8, 8, LANES), axis=0)
                total_at[...] += mix(values[pl.ds(at, count)].reshape(count * ROWS, HD), weights)

            def plain(i, c):
                step(i * MAIN, MAIN, False)
                return c

            def masked(i, c):
                step(i * MAIN, MAIN, True)
                return c

            open_steps = jnp.right_shift(lowest, MAIN.bit_length() - 1)
            steps = jnp.right_shift(highest, MAIN.bit_length() - 1)
            lax.fori_loop(0, open_steps, plain, 0)
            lax.fori_loop(open_steps, steps, masked, 0)
            rest = highest - steps * MAIN
            below = 0
            for count in LAST:

                @pl.when((rest > below) & (rest <= count))
                def _():
                    step(steps * MAIN, count, True, True)

                below = count

            if not first:
                counted = counted_of(tile)
                whole = jnp.sum(sums[...], axis=0, keepdims=True)
                safe = (whole >= LOW) & (whole <= HIGH)
                unsafe[...] = jnp.maximum(unsafe[...], jnp.where(counted & jnp.logical_not(safe), 1.0, 0.0))
                sums[0:1, :] = whole
                finish(tile, counted)
            return needed

        arrived = lax.fori_loop(0, tiles, visit, jnp.int32(0))
        if first:
            return
        lax.fori_loop(arrived, groups, arrive, 0)

        @pl.when(jnp.max(unsafe[...]) > 0.0)
        def _():
            def again(tile, carry):
                take_queries(tile)
                counted = counted_of(tile)
                ranks = lanes[tile, 5:6, :]
                rank = table[RANK + tile * TILE + TILE - 1]
                peak[...] = jnp.full_like(peak, -1e30)
                total[...] = jnp.zeros_like(total)
                sums[...] = jnp.zeros_like(sums)

                def of_group(p, c):
                    j = table[PLACE + p]
                    for side in range(2):

                        def careful(s, c, side=side):
                            block = jnp.where(
                                parity == side,
                                own[j * per_group + s, ROWS : 3 * ROWS],
                                landed[p * per_group + s],
                            )
                            row = lax.broadcasted_iota(jnp.int32, (ROWS, LANES), 0)
                            within = (row < valid[j] - (2 * s + side) * ROWS) & (p <= ranks)
                            scores = jnp.where(within, scores_of(block[0:ROWS]), -1e30)
                            before = peak[...]
                            now = jnp.maximum(before, jnp.max(scores, axis=0, keepdims=True))
                            shrink = jnp.exp2(before - now)
                            weights = jnp.where(within, jnp.exp2(scores - now), 0.0)
                            sums[0:1, :] = sums[0:1, :] * shrink + jnp.sum(weights, axis=0, keepdims=True)
                            total[...] = total[...] * shrink + mix(block[ROWS : 2 * ROWS], weights)
                            peak[...] = now
                            return c

                        lax.fori_loop(0, jnp.right_shift(all_blocks(j) + 1 - side, 1), careful, 0)
                    return c

                lax.fori_loop(0, rank + 1, of_group, 0)
                finish(tile, counted)
                return carry

            lax.fori_loop(0, tiles, again, 0)

    if not first:

        @pl.when(active == 0)
        def _():
            out[...] = jnp.zeros_like(out)


def attend_call(table, valid, lanes, own, other, state):
    first = other is None
    slots = own.shape[0]
    groups = valid.shape[0]
    smem = pl.BlockSpec(memory_space=pltpu.SMEM)
    vmem = pl.BlockSpec(memory_space=pltpu.VMEM)
    hbm = pl.BlockSpec(memory_space=pltpu.HBM)
    packed = pltpu.VMEM((slots + TILE, ROWS, HD), jnp.bfloat16)
    scratch = [packed, packed, pltpu.VMEM((TILE, ROWS, HD), jnp.bfloat16)]
    work = slots * ROWS * slots * ROWS // 2
    if first:
        tiles = slots // TILE
        operands, specs = (own,), [vmem]
        shapes = (
            jax.ShapeDtypeStruct((tiles, HD, LANES), jnp.float32),
            jax.ShapeDtypeStruct((tiles, 8, LANES), jnp.float32),
        )
        out_specs = (vmem, vmem)
    else:
        operands, specs = (own, other, *state), [vmem, hbm, vmem, vmem]
        shapes = jax.ShapeDtypeStruct((slots, ROWS, HD), jnp.bfloat16)
        out_specs = vmem
        scratch += [
            pltpu.VMEM((slots, 2 * ROWS, HD), jnp.bfloat16),
            pltpu.VMEM((HD, LANES), jnp.float32),
            pltpu.VMEM((8, LANES), jnp.float32),
            pltpu.VMEM((1, LANES), jnp.float32),
            pltpu.VMEM((1, LANES), jnp.float32),
            pltpu.SemaphoreType.DMA((groups,)),
        ]
    return pl.pallas_call(
        functools.partial(attend_kernel, first),
        out_shape=shapes,
        in_specs=[smem, smem, vmem, *specs],
        out_specs=out_specs,
        scratch_shapes=scratch,
        compiler_params=pltpu.CompilerParams(vmem_limit_bytes=36 * 2**20),
        cost_estimate=pl.CostEstimate(flops=4 * HD * work, bytes_accessed=8 * 2**20, transcendentals=work),
    )(table, valid, lanes, *operands)


def attend(table, valid, lanes, own, other):
    state = attend_call(table, valid, lanes, own, None, ())
    return attend_call(table, valid, lanes, own, other, state)


def plan(order, valid, parity, per_group, table):
    groups = order.shape[0]
    for j in range(groups):
        table[PLACE + order[j]] = j
    starts = [jnp.int32(0), jnp.int32(0)]
    gaps = [jnp.int32(0), jnp.int32(0)]
    held = jnp.int32(0)
    for j in range(groups):
        held = held + jnp.right_shift(jnp.right_shift(valid[j] + ROWS - 1, SHIFT) + 1 - parity, 1)
    tiles = jnp.right_shift(held + TILE - 1, TILE.bit_length() - 1)
    pad = tiles * TILE - held
    table[TILES], table[PAD] = tiles, pad
    filled = pad
    for p in range(groups):
        j = table[PLACE + p]
        blocks = jnp.right_shift(valid[j] + ROWS - 1, SHIFT)
        gap = blocks * ROWS - valid[j]
        last_core = jnp.bitwise_and(blocks - 1, 1)
        counts = [jnp.right_shift(blocks + 1 - core, 1) for core in (parity, 1 - parity)]
        for which, core in enumerate((parity, 1 - parity)):
            table[STARTS[which] + p] = starts[which]
            starts[which] = starts[which] + counts[which]
            gaps[which] = gaps[which] + jnp.where(last_core == core, gap, 0)
        for i in range(per_group):
            at = filled + i
            table[SLOT + at] = j * per_group + i
            table[LEFT + at] = valid[j] - (2 * i + parity) * ROWS
            table[RANK + at] = p
            for which in range(2):
                table[END[which] + at] = starts[which]
                table[GAP[which] + at] = gaps[which]
        filled = filled + counts[0]
    for which in range(2):
        table[STARTS[which] + groups] = starts[which]
    for i in range(TILE):
        front = i < pad
        table[SLOT + i] = jnp.where(front, table[SLOT + pad], table[SLOT + i])
        table[LEFT + i] = jnp.where(front, 0, table[LEFT + i])
        table[RANK + i] = jnp.where(front, table[RANK + pad], table[RANK + i])
        for base in (*END, *GAP):
            table[base + i] = jnp.where(front, table[base + pad], table[base + i])


def describe_tiles(table, lanes):
    def describe(tile, carry):
        for i in range(TILE):
            for n, base in enumerate((END[0], END[1], GAP[0], GAP[1], LEFT, RANK)):
                of_block = jnp.full((1, ROWS), table[base + tile * TILE + i], jnp.int32)
                lanes[tile, n : n + 1, i * ROWS : (i + 1) * ROWS] = of_block
        return carry

    lax.fori_loop(0, table[TILES], describe, 0)


def split_kernel(heads, order, valid, query_rows, key_rows, value_rows, out, table_out, lanes_out, *scratch):
    staged, order_here, valid_here, table, lanes, taken, given, read, written = scratch
    inputs = (query_rows, key_rows, value_rows)
    small = [
        pltpu.make_async_copy(order, order_here, read.at[0]),
        pltpu.make_async_copy(valid, valid_here, read.at[1]),
    ]
    arrivals = [pltpu.make_async_copy(rows.at[0], staged.at[n], taken.at[n]) for n, rows in enumerate(inputs)]
    for copy in (*small, *arrivals):
        copy.start()
    for copy in small:
        copy.wait()
    parity = jnp.bitwise_and(lax.axis_index("head"), 1)
    chip = (lax.axis_index("group") * lax.axis_size("head") + lax.axis_index("head") - parity) // 2
    table[PARITY], table[ACTIVE] = parity, (chip < heads).astype(jnp.int32)
    plan(order_here, valid_here, parity, lanes.shape[0] * TILE // order.shape[0], table)
    table_gone = pltpu.make_async_copy(table, table_out, written.at[0])
    table_gone.start()
    for n, copy in enumerate(arrivals):
        copy.wait()
        for h in range(heads):
            pltpu.make_async_copy(
                staged.at[n, :, h * HD : (h + 1) * HD], out.at[h, n * ROWS : (n + 1) * ROWS], given
            ).start()
    describe_tiles(table, lanes)
    lanes_gone = pltpu.make_async_copy(lanes, lanes_out, written.at[1])
    lanes_gone.start()
    everything = out.at[0:heads]
    pltpu.make_async_copy(everything, everything, given).wait()
    table_gone.wait()
    lanes_gone.wait()


def split_heads(slots, order, valid, query_rows, key_rows, value_rows):
    hbm = pl.BlockSpec(memory_space=pltpu.HBM)
    return pl.pallas_call(
        functools.partial(split_kernel, query_rows.shape[2] // HD),
        out_shape=(
            jax.ShapeDtypeStruct((slots, 3 * ROWS, HD), query_rows.dtype),
            jax.ShapeDtypeStruct((SIZE,), jnp.int32),
            jax.ShapeDtypeStruct((slots // TILE, 8, LANES), jnp.int32),
        ),
        in_specs=[hbm] * 5,
        out_specs=(hbm,) * 3,
        scratch_shapes=[
            pltpu.VMEM((3, *query_rows.shape[1:]), query_rows.dtype),
            pltpu.SMEM(order.shape, jnp.int32),
            pltpu.SMEM(valid.shape, jnp.int32),
            pltpu.SMEM((SIZE,), jnp.int32),
            pltpu.VMEM((slots // TILE, 8, LANES), jnp.int32),
            pltpu.SemaphoreType.DMA((3,)),
            pltpu.SemaphoreType.DMA,
            pltpu.SemaphoreType.DMA((2,)),
            pltpu.SemaphoreType.DMA((2,)),
        ],
        compiler_params=pltpu.CompilerParams(vmem_limit_bytes=61 * 2**20),
    )(order, valid, query_rows, key_rows, value_rows)


def join_kernel(heads, attended, out, sem):
    for h in range(heads):
        pltpu.make_async_copy(attended.at[h], out.at[0, :, h * HD : (h + 1) * HD], sem).start()
    pltpu.make_async_copy(out, out, sem).wait()


def join_heads(heads, attended):
    return pl.pallas_call(
        functools.partial(join_kernel, heads),
        out_shape=jax.ShapeDtypeStruct((1, ROWS, heads * HD), attended.dtype),
        in_specs=[pl.BlockSpec(memory_space=pltpu.VMEM)],
        out_specs=pl.BlockSpec(memory_space=pltpu.HBM),
        scratch_shapes=[pltpu.SemaphoreType.DMA],
        compiler_params=pltpu.CompilerParams(vmem_limit_bytes=8 * 2**20),
    )(attended)


def body(query_rows, key_rows, value_rows, group_order, valid_counts):
    groups, cores = lax.axis_size("group"), lax.axis_size("head")
    devices = groups * cores
    slots = devices // 2
    heads = query_rows.shape[2] // HD
    same_core = [[i for i in range(devices) if i % 2 == core] for core in range(2)]

    def exchange(x):
        return lax.all_to_all(x, ("group", "head"), 0, 0, axis_index_groups=same_core, tiled=True)

    sent, table, lanes = split_heads(slots, group_order, valid_counts, query_rows, key_rows, value_rows)
    own = exchange(sent)
    other = lax.ppermute(own, "head", [(i, i ^ 1) for i in range(cores)])
    attended = attend(table, valid_counts, lanes, own, other)
    return join_heads(heads, exchange(attended))


def solution(mesh):
    placed = (
        P("group", "head", None),
        P("group", "head", None),
        P("group", "head", None),
        P(),
        P(),
    )
    return jax.shard_map(
        body, mesh=mesh, in_specs=placed, out_specs=P("group", "head", None), check_vma=False
    )
```

```python
import functools
import math

import jax
import jax.numpy as jnp
from jax import lax
from jax.experimental import pallas as pl
from jax.experimental.pallas import tpu as pltpu
from jax.sharding import PartitionSpec as P

HD = 128
ROWS = 64
TILE = 12
LANES = TILE * ROWS
STEPS = (8, 16, 24, 32, 40, 48, 56, 64)
SHIFT = ROWS.bit_length() - 1
PLACE, TILES, PAD, PARITY, ACTIVE, STARTS = 0, 8, 9, 10, 11, (16, 32)
SLOT, LEFT, RANK, END, GAP = 48, 128, 208, (288, 368), (448, 528)
SIZE = 608
EDGE = 32
SCALE = HD ** (-0.5)
LOG2E = math.log2(math.e)
LOW, HIGH = 1.0, 2.0**110


def attend_kernel(first, *refs):
    if first:
        table, valid, lanes, own, total_out, sums_out, *scratch = refs
        keys, values, queries, total, sums = scratch
    else:
        table, valid, lanes, own, other, total_in, sums_in, out, *scratch = refs
        keys, values, queries, total, sums, peak, unsafe = scratch
    parity, active = table[PARITY], table[ACTIVE]
    which = 0 if first else 1
    core = parity if first else 1 - parity
    groups = valid.shape[0]
    per_group = own.shape[0] // groups

    def all_blocks(j):
        return jnp.right_shift(valid[j] + ROWS - 1, SHIFT)

    @pl.when(active == 1)
    def _():
        if not first:
            out[...] = jnp.zeros_like(out)
            unsafe[...] = jnp.zeros_like(unsafe)
        tiles, pad = table[TILES], table[PAD]

        def arrive(p, carry):
            j = table[PLACE + p]
            at = table[STARTS[which] + p]
            slab = (own if first else other)[pl.ds(j * per_group, per_group), ROWS : 3 * ROWS]
            keys[pl.ds(at, per_group)] = slab[:, 0:ROWS]
            values[pl.ds(at, per_group)] = slab[:, ROWS : 2 * ROWS]
            blocks = all_blocks(j)

            @pl.when(jnp.bitwise_and(blocks - 1, 1) == core)
            def _():
                block = table[STARTS[which] + p + 1] - 1
                there = lax.broadcasted_iota(jnp.int32, (ROWS, HD), 0) < valid[j] - (blocks - 1) * ROWS
                for ref in (keys, values):
                    rows = ref[block]
                    ref[block] = jnp.where(there, rows, jnp.zeros_like(rows))

            @pl.when(p == groups - 1)
            def _():
                for ref in (keys, values):
                    ref[pl.ds(table[STARTS[which] + groups], TILE)] = jnp.zeros((TILE, ROWS, HD), jnp.bfloat16)

            return carry

        def scores_of(rows):
            return (
                lax.dot_general(
                    rows,
                    queries[...].reshape(LANES, HD),
                    (((1,), (1,)), ((), ())),
                    preferred_element_type=jnp.float32,
                )
                * (SCALE * LOG2E)
            )

        def mix(rows, weights):
            return lax.dot_general(
                rows,
                weights.astype(jnp.bfloat16),
                (((0,), (0,)), ((), ())),
                preferred_element_type=jnp.float32,
            )

        def take_queries(tile):
            for i in range(TILE):
                queries[i] = own[table[SLOT + tile * TILE + i], 0:ROWS]

        def counted_of(tile):
            row = jnp.bitwise_and(lax.broadcasted_iota(jnp.int32, (1, LANES), 1), ROWS - 1)
            return row < lanes[tile, 4:5, :]

        def finish(tile, counted):
            result = jnp.where(counted, total[...] * (1.0 / sums[0:1, :]), 0.0)
            result = result.astype(jnp.bfloat16).T
            for i in range(TILE):

                @pl.when(tile * TILE + i >= pad)
                def _():
                    out[table[SLOT + tile * TILE + i]] = result[i * ROWS : (i + 1) * ROWS, :]

        def visit(tile, arrived):
            take_queries(tile)
            limit = lanes[tile, which : which + 1, :]
            gap = lanes[tile, 2 + which : 3 + which, :]
            highest = table[END[which] + tile * TILE + TILE - 1]
            rank = table[RANK + tile * TILE + TILE - 1]
            needed = jnp.minimum(rank + 3, groups)
            lax.fori_loop(arrived, needed, arrive, 0)
            lead = lax.broadcasted_iota(jnp.int32, (8, LANES), 0) == 0
            missing = jnp.where(lead, -gap.astype(jnp.float32), 0.0)
            if first:
                total[...] = jnp.zeros_like(total)
                sums[...] = missing
            else:
                total[...] = total_in[tile]
                sums[...] = sums_in[tile] + missing

            def step(count):
                scores = scores_of(keys[0:count].reshape(count * ROWS, HD))
                edge = min(count, EDGE)
                open_rows = (count - edge) * ROWS
                block = lax.broadcasted_iota(jnp.int32, (edge, 1, LANES), 0) + (count - edge)
                bias = jnp.where(block < limit.reshape(1, 1, LANES), 0.0, -1e30)
                shut = (scores[open_rows:].reshape(edge, ROWS, LANES) + bias).reshape(edge * ROWS, LANES)
                scores = jnp.concatenate([scores[:open_rows], shut], axis=0) if open_rows else shut
                weights = jnp.exp2(scores)
                sums[...] += jnp.sum(weights.reshape(count * ROWS // 8, 8, LANES), axis=0)
                total[...] += mix(values[0:count].reshape(count * ROWS, HD), weights)

            below = 0
            for count in STEPS:

                @pl.when((highest > below) & (highest <= count))
                def _():
                    step(count)

                below = count

            if first:
                total_out[tile] = total[...]
                sums_out[tile] = sums[...]
            else:
                counted = counted_of(tile)
                whole = jnp.sum(sums[...], axis=0, keepdims=True)
                safe = (whole >= LOW) & (whole <= HIGH)
                unsafe[...] = jnp.maximum(unsafe[...], jnp.where(counted & jnp.logical_not(safe), 1.0, 0.0))
                sums[0:1, :] = whole
                finish(tile, counted)
            return needed

        lax.fori_loop(0, tiles, visit, jnp.int32(0))
        if first:
            return
        @pl.when(jnp.max(unsafe[...]) > 0.0)
        def _():
            def again(tile, carry):
                take_queries(tile)
                counted = counted_of(tile)
                ranks = lanes[tile, 5:6, :]
                rank = table[RANK + tile * TILE + TILE - 1]
                peak[...] = jnp.full_like(peak, -1e30)
                total[...] = jnp.zeros_like(total)
                sums[...] = jnp.zeros_like(sums)

                def of_group(p, c):
                    j = table[PLACE + p]
                    for side in range(2):

                        def careful(s, c, side=side):
                            block = jnp.where(
                                parity == side,
                                own[j * per_group + s, ROWS : 3 * ROWS],
                                other[j * per_group + s, ROWS : 3 * ROWS],
                            )
                            row = lax.broadcasted_iota(jnp.int32, (ROWS, LANES), 0)
                            within = (row < valid[j] - (2 * s + side) * ROWS) & (p <= ranks)
                            scores = jnp.where(within, scores_of(block[0:ROWS]), -1e30)
                            before = peak[...]
                            now = jnp.maximum(before, jnp.max(scores, axis=0, keepdims=True))
                            shrink = jnp.exp2(before - now)
                            weights = jnp.where(within, jnp.exp2(scores - now), 0.0)
                            sums[0:1, :] = sums[0:1, :] * shrink + jnp.sum(weights, axis=0, keepdims=True)
                            total[...] = total[...] * shrink + mix(block[ROWS : 2 * ROWS], weights)
                            peak[...] = now
                            return c

                        lax.fori_loop(0, jnp.right_shift(all_blocks(j) + 1 - side, 1), careful, 0)
                    return c

                lax.fori_loop(0, rank + 1, of_group, 0)
                finish(tile, counted)
                return carry

            lax.fori_loop(0, tiles, again, 0)

    if not first:

        @pl.when(active == 0)
        def _():
            out[...] = jnp.zeros_like(out)


def attend_call(table, valid, lanes, own, other, state):
    first = other is None
    slots = own.shape[0]
    groups = valid.shape[0]
    assert slots <= STEPS[-1]
    smem = pl.BlockSpec(memory_space=pltpu.SMEM)
    vmem = pl.BlockSpec(memory_space=pltpu.VMEM)
    packed = pltpu.VMEM((slots + TILE, ROWS, HD), jnp.bfloat16)
    scratch = [
        packed,
        packed,
        pltpu.VMEM((TILE, ROWS, HD), jnp.bfloat16),
        pltpu.VMEM((HD, LANES), jnp.float32),
        pltpu.VMEM((8, LANES), jnp.float32),
    ]
    work = slots * ROWS * slots * ROWS // 2
    if first:
        tiles = pl.cdiv(slots, TILE)
        operands, specs = (own,), [vmem]
        shapes = (
            jax.ShapeDtypeStruct((tiles, HD, LANES), jnp.float32),
            jax.ShapeDtypeStruct((tiles, 8, LANES), jnp.float32),
        )
        out_specs = (vmem, vmem)
    else:
        operands, specs = (own, other, *state), [vmem, vmem, vmem, vmem]
        shapes = jax.ShapeDtypeStruct((slots, ROWS, HD), jnp.bfloat16)
        out_specs = vmem
        scratch += [pltpu.VMEM((1, LANES), jnp.float32)] * 2
    return pl.pallas_call(
        functools.partial(attend_kernel, first),
        out_shape=shapes,
        in_specs=[smem, smem, vmem, *specs],
        out_specs=out_specs,
        scratch_shapes=scratch,
        compiler_params=pltpu.CompilerParams(vmem_limit_bytes=44 * 2**20),
        cost_estimate=pl.CostEstimate(flops=4 * HD * work, bytes_accessed=8 * 2**20, transcendentals=work),
    )(table, valid, lanes, *operands)


def attend(table, valid, lanes, own, other):
    state = attend_call(table, valid, lanes, own, None, ())
    return attend_call(table, valid, lanes, own, other, state)


def plan(order, valid, parity, per_group, table):
    groups = order.shape[0]
    for j in range(groups):
        table[PLACE + order[j]] = j
    starts = [jnp.int32(0), jnp.int32(0)]
    gaps = [jnp.int32(0), jnp.int32(0)]
    held = jnp.int32(0)
    for j in range(groups):
        held = held + jnp.right_shift(jnp.right_shift(valid[j] + ROWS - 1, SHIFT) + 1 - parity, 1)
    tiles = lax.div(held + TILE - 1, jnp.int32(TILE))
    pad = tiles * TILE - held
    table[TILES], table[PAD] = tiles, pad
    filled = pad
    for p in range(groups):
        j = table[PLACE + p]
        blocks = jnp.right_shift(valid[j] + ROWS - 1, SHIFT)
        gap = blocks * ROWS - valid[j]
        last_core = jnp.bitwise_and(blocks - 1, 1)
        counts = [jnp.right_shift(blocks + 1 - core, 1) for core in (parity, 1 - parity)]
        for which, core in enumerate((parity, 1 - parity)):
            table[STARTS[which] + p] = starts[which]
            starts[which] = starts[which] + counts[which]
            gaps[which] = gaps[which] + jnp.where(last_core == core, gap, 0)
        for i in range(per_group):
            at = filled + i
            table[SLOT + at] = j * per_group + i
            table[LEFT + at] = valid[j] - (2 * i + parity) * ROWS
            table[RANK + at] = p
            for which in range(2):
                table[END[which] + at] = starts[which]
                table[GAP[which] + at] = gaps[which]
        filled = filled + counts[0]
    for which in range(2):
        table[STARTS[which] + groups] = starts[which]
    for i in range(TILE):
        front = i < pad
        table[SLOT + i] = jnp.where(front, table[SLOT + pad], table[SLOT + i])
        table[LEFT + i] = jnp.where(front, 0, table[LEFT + i])
        table[RANK + i] = jnp.where(front, table[RANK + pad], table[RANK + i])
        for base in (*END, *GAP):
            table[base + i] = jnp.where(front, table[base + pad], table[base + i])


def describe_tiles(table, lanes):
    def describe(tile, carry):
        for i in range(TILE):
            for n, base in enumerate((END[0], END[1], GAP[0], GAP[1], LEFT, RANK)):
                of_block = jnp.full((1, ROWS), table[base + tile * TILE + i], jnp.int32)
                lanes[tile, n : n + 1, i * ROWS : (i + 1) * ROWS] = of_block
        return carry

    lax.fori_loop(0, table[TILES], describe, 0)


def split_kernel(heads, order, valid, query_rows, key_rows, value_rows, out, table_out, lanes_out, *scratch):
    staged, order_here, valid_here, table, lanes, taken, given, read, written = scratch
    inputs = (query_rows, key_rows, value_rows)
    small = [
        pltpu.make_async_copy(order, order_here, read.at[0]),
        pltpu.make_async_copy(valid, valid_here, read.at[1]),
    ]
    arrivals = [pltpu.make_async_copy(rows.at[0], staged.at[n], taken.at[n]) for n, rows in enumerate(inputs)]
    for copy in (*small, *arrivals):
        copy.start()
    for copy in small:
        copy.wait()
    slots = out.shape[0]
    parity = jnp.bitwise_and(lax.axis_index("head"), 1)
    chip = (lax.axis_index("group") * lax.axis_size("head") + lax.axis_index("head") - parity) // 2
    table[PARITY], table[ACTIVE] = parity, (chip < heads).astype(jnp.int32)
    plan(order_here, valid_here, parity, slots // order.shape[0], table)
    table_gone = pltpu.make_async_copy(table, table_out, written.at[0])
    table_gone.start()
    for n, copy in enumerate(arrivals):
        copy.wait()
        for h in range(heads):
            pltpu.make_async_copy(
                staged.at[n, :, h * HD : (h + 1) * HD], out.at[h, n * ROWS : (n + 1) * ROWS], given
            ).start()
    describe_tiles(table, lanes)
    lanes_gone = pltpu.make_async_copy(lanes, lanes_out, written.at[1])
    lanes_gone.start()
    everything = out.at[0:heads]
    pltpu.make_async_copy(everything, everything, given).wait()
    table_gone.wait()
    lanes_gone.wait()


def split_heads(slots, order, valid, query_rows, key_rows, value_rows):
    hbm = pl.BlockSpec(memory_space=pltpu.HBM)
    return pl.pallas_call(
        functools.partial(split_kernel, query_rows.shape[2] // HD),
        out_shape=(
            jax.ShapeDtypeStruct((slots, 3 * ROWS, HD), query_rows.dtype),
            jax.ShapeDtypeStruct((SIZE,), jnp.int32),
            jax.ShapeDtypeStruct((pl.cdiv(slots, TILE), 8, LANES), jnp.int32),
        ),
        in_specs=[hbm] * 5,
        out_specs=(hbm,) * 3,
        scratch_shapes=[
            pltpu.VMEM((3, *query_rows.shape[1:]), query_rows.dtype),
            pltpu.SMEM(order.shape, jnp.int32),
            pltpu.SMEM(valid.shape, jnp.int32),
            pltpu.SMEM((SIZE,), jnp.int32),
            pltpu.VMEM((pl.cdiv(slots, TILE), 8, LANES), jnp.int32),
            pltpu.SemaphoreType.DMA((3,)),
            pltpu.SemaphoreType.DMA,
            pltpu.SemaphoreType.DMA((2,)),
            pltpu.SemaphoreType.DMA((2,)),
        ],
        compiler_params=pltpu.CompilerParams(vmem_limit_bytes=61 * 2**20),
    )(order, valid, query_rows, key_rows, value_rows)


def join_kernel(heads, attended, out, sem):
    for h in range(heads):
        pltpu.make_async_copy(attended.at[h], out.at[0, :, h * HD : (h + 1) * HD], sem).start()
    pltpu.make_async_copy(out, out, sem).wait()


def join_heads(heads, attended):
    return pl.pallas_call(
        functools.partial(join_kernel, heads),
        out_shape=jax.ShapeDtypeStruct((1, ROWS, heads * HD), attended.dtype),
        in_specs=[pl.BlockSpec(memory_space=pltpu.VMEM)],
        out_specs=pl.BlockSpec(memory_space=pltpu.HBM),
        scratch_shapes=[pltpu.SemaphoreType.DMA],
        compiler_params=pltpu.CompilerParams(vmem_limit_bytes=8 * 2**20),
    )(attended)


def body(query_rows, key_rows, value_rows, group_order, valid_counts):
    groups, cores = lax.axis_size("group"), lax.axis_size("head")
    devices = groups * cores
    slots = devices // 2
    heads = query_rows.shape[2] // HD
    same_core = [[i for i in range(devices) if i % 2 == core] for core in range(2)]

    def exchange(x):
        return lax.all_to_all(x, ("group", "head"), 0, 0, axis_index_groups=same_core, tiled=True)

    sent, table, lanes = split_heads(slots, group_order, valid_counts, query_rows, key_rows, value_rows)
    own = exchange(sent)
    other = lax.ppermute(own, "head", [(i, i ^ 1) for i in range(cores)])
    attended = attend(table, valid_counts, lanes, own, other)
    return join_heads(heads, exchange(attended))


def solution(mesh):
    placed = (
        P("group", "head", None),
        P("group", "head", None),
        P("group", "head", None),
        P(),
        P(),
    )
    return jax.shard_map(
        body, mesh=mesh, in_specs=placed, out_specs=P("group", "head", None), check_vma=False
    )
```

```python
import functools
import math

import jax
import jax.numpy as jnp
from jax import lax
from jax.experimental import pallas as pl
from jax.experimental.pallas import tpu as pltpu
from jax.sharding import PartitionSpec as P

HD = 128
ROWS = 64
TILE = 12
LANES = TILE * ROWS
STEPS = (8, 16, 24, 32, 40, 48, 56, 64)
SHIFT = ROWS.bit_length() - 1
PLACE, TILES, PAD, PARITY, ACTIVE, STARTS = 0, 8, 9, 10, 11, (16, 32)
SLOT, LEFT, RANK, END, GAP = 48, 128, 208, (288, 368), (448, 528)
SIZE = 608
EDGE = 32
SCALE = HD ** (-0.5)
LOG2E = math.log2(math.e)
LOW, HIGH = 1.0, 2.0**110


def attend_kernel(first, *refs):
    if first:
        table, valid, lanes, own, total_out, sums_out, *scratch = refs
        keys, values, queries, total, sums = scratch
    else:
        table, valid, lanes, own, other, total_in, sums_in, out, *scratch = refs
        keys, values, queries, total, sums, peak, unsafe = scratch
    parity, active = table[PARITY], table[ACTIVE]
    which = 0 if first else 1
    core = parity if first else 1 - parity
    groups = valid.shape[0]
    per_group = own.shape[0] // groups

    def all_blocks(j):
        return jnp.right_shift(valid[j] + ROWS - 1, SHIFT)

    @pl.when(active == 1)
    def _():
        if not first:
            out[...] = jnp.zeros_like(out)
            unsafe[...] = jnp.zeros_like(unsafe)
        tiles, pad = table[TILES], table[PAD]

        def arrive(p, carry):
            j = table[PLACE + p]
            at = table[STARTS[which] + p]
            slab = (own if first else other)[pl.ds(j * per_group, per_group), ROWS : 3 * ROWS]
            keys[pl.ds(at, per_group)] = slab[:, 0:ROWS]
            values[pl.ds(at, per_group)] = slab[:, ROWS : 2 * ROWS]
            blocks = all_blocks(j)

            @pl.when(jnp.bitwise_and(blocks - 1, 1) == core)
            def _():
                block = table[STARTS[which] + p + 1] - 1
                there = lax.broadcasted_iota(jnp.int32, (ROWS, HD), 0) < valid[j] - (blocks - 1) * ROWS
                for ref in (keys, values):
                    rows = ref[block]
                    ref[block] = jnp.where(there, rows, jnp.zeros_like(rows))

            @pl.when(p == groups - 1)
            def _():
                for ref in (keys, values):
                    ref[pl.ds(table[STARTS[which] + groups], TILE)] = jnp.zeros((TILE, ROWS, HD), jnp.bfloat16)

            return carry

        def scores_of(rows):
            return (
                lax.dot_general(
                    rows,
                    queries[...].reshape(LANES, HD),
                    (((1,), (1,)), ((), ())),
                    preferred_element_type=jnp.float32,
                )
                * (SCALE * LOG2E)
            )

        def mix(rows, weights):
            return lax.dot_general(
                rows,
                weights.astype(jnp.bfloat16),
                (((0,), (0,)), ((), ())),
                preferred_element_type=jnp.float32,
            )

        def take_queries(tile):
            for i in range(TILE):
                queries[i] = own[table[SLOT + tile * TILE + i], 0:ROWS]

        def counted_of(tile):
            row = jnp.bitwise_and(lax.broadcasted_iota(jnp.int32, (1, LANES), 1), ROWS - 1)
            return row < lanes[tile, 4:5, :]

        def finish(tile, counted):
            result = jnp.where(counted, total[...] * (1.0 / sums[0:1, :]), 0.0)
            result = result.astype(jnp.bfloat16).T
            for i in range(TILE):

                @pl.when(tile * TILE + i >= pad)
                def _():
                    out[table[SLOT + tile * TILE + i]] = result[i * ROWS : (i + 1) * ROWS, :]

        def visit(tile, arrived):
            take_queries(tile)
            limit = lanes[tile, which : which + 1, :]
            gap = lanes[tile, 2 + which : 3 + which, :]
            highest = table[END[which] + tile * TILE + TILE - 1]
            rank = table[RANK + tile * TILE + TILE - 1]
            needed = jnp.minimum(rank + 3, groups)
            lax.fori_loop(arrived, needed, arrive, 0)
            lead = lax.broadcasted_iota(jnp.int32, (8, LANES), 0) == 0
            missing = jnp.where(lead, -gap.astype(jnp.float32), 0.0)
            def step(count):
                scores = scores_of(keys[0:count].reshape(count * ROWS, HD))
                edge = min(count, EDGE)
                open_rows = (count - edge) * ROWS
                block = lax.broadcasted_iota(jnp.int32, (edge, 1, LANES), 0) + (count - edge)
                bias = jnp.where(block < limit.reshape(1, 1, LANES), 0.0, -1e30)
                shut = (scores[open_rows:].reshape(edge, ROWS, LANES) + bias).reshape(edge * ROWS, LANES)
                scores = jnp.concatenate([scores[:open_rows], shut], axis=0) if open_rows else shut
                weights = jnp.exp2(scores)
                summed = missing + jnp.sum(weights.reshape(count * ROWS // 8, 8, LANES), axis=0)
                mixed = mix(values[0:count].reshape(count * ROWS, HD), weights)
                if first:
                    sums_out[tile] = summed
                    total_out[tile] = mixed
                else:
                    sums[...] = sums_in[tile] + summed
                    total[...] = total_in[tile] + mixed

            below = 0
            for count in STEPS:

                @pl.when((highest > below) & (highest <= count))
                def _():
                    step(count)

                below = count

            if not first:
                counted = counted_of(tile)
                whole = jnp.sum(sums[...], axis=0, keepdims=True)
                safe = (whole >= LOW) & (whole <= HIGH)
                unsafe[...] = jnp.maximum(unsafe[...], jnp.where(counted & jnp.logical_not(safe), 1.0, 0.0))
                sums[0:1, :] = whole
                finish(tile, counted)
            return needed

        lax.fori_loop(0, tiles, visit, jnp.int32(0))
        if first:
            return
        @pl.when(jnp.max(unsafe[...]) > 0.0)
        def _():
            def again(tile, carry):
                take_queries(tile)
                counted = counted_of(tile)
                ranks = lanes[tile, 5:6, :]
                rank = table[RANK + tile * TILE + TILE - 1]
                peak[...] = jnp.full_like(peak, -1e30)
                total[...] = jnp.zeros_like(total)
                sums[...] = jnp.zeros_like(sums)

                def of_group(p, c):
                    j = table[PLACE + p]
                    for side in range(2):

                        def careful(s, c, side=side):
                            block = jnp.where(
                                parity == side,
                                own[j * per_group + s, ROWS : 3 * ROWS],
                                other[j * per_group + s, ROWS : 3 * ROWS],
                            )
                            row = lax.broadcasted_iota(jnp.int32, (ROWS, LANES), 0)
                            within = (row < valid[j] - (2 * s + side) * ROWS) & (p <= ranks)
                            scores = jnp.where(within, scores_of(block[0:ROWS]), -1e30)
                            before = peak[...]
                            now = jnp.maximum(before, jnp.max(scores, axis=0, keepdims=True))
                            shrink = jnp.exp2(before - now)
                            weights = jnp.where(within, jnp.exp2(scores - now), 0.0)
                            sums[0:1, :] = sums[0:1, :] * shrink + jnp.sum(weights, axis=0, keepdims=True)
                            total[...] = total[...] * shrink + mix(block[ROWS : 2 * ROWS], weights)
                            peak[...] = now
                            return c

                        lax.fori_loop(0, jnp.right_shift(all_blocks(j) + 1 - side, 1), careful, 0)
                    return c

                lax.fori_loop(0, rank + 1, of_group, 0)
                finish(tile, counted)
                return carry

            lax.fori_loop(0, tiles, again, 0)

    if not first:

        @pl.when(active == 0)
        def _():
            out[...] = jnp.zeros_like(out)


def attend_call(table, valid, lanes, own, other, state):
    first = other is None
    slots = own.shape[0]
    groups = valid.shape[0]
    assert slots <= STEPS[-1]
    smem = pl.BlockSpec(memory_space=pltpu.SMEM)
    vmem = pl.BlockSpec(memory_space=pltpu.VMEM)
    packed = pltpu.VMEM((slots + TILE, ROWS, HD), jnp.bfloat16)
    scratch = [
        packed,
        packed,
        pltpu.VMEM((TILE, ROWS, HD), jnp.bfloat16),
        pltpu.VMEM((HD, LANES), jnp.float32),
        pltpu.VMEM((8, LANES), jnp.float32),
    ]
    work = slots * ROWS * slots * ROWS // 2
    if first:
        tiles = pl.cdiv(slots, TILE)
        operands, specs = (own,), [vmem]
        shapes = (
            jax.ShapeDtypeStruct((tiles, HD, LANES), jnp.float32),
            jax.ShapeDtypeStruct((tiles, 8, LANES), jnp.float32),
        )
        out_specs = (vmem, vmem)
    else:
        operands, specs = (own, other, *state), [vmem, vmem, vmem, vmem]
        shapes = jax.ShapeDtypeStruct((slots, ROWS, HD), jnp.bfloat16)
        out_specs = vmem
        scratch += [pltpu.VMEM((1, LANES), jnp.float32)] * 2
    return pl.pallas_call(
        functools.partial(attend_kernel, first),
        out_shape=shapes,
        in_specs=[smem, smem, vmem, *specs],
        out_specs=out_specs,
        scratch_shapes=scratch,
        compiler_params=pltpu.CompilerParams(vmem_limit_bytes=44 * 2**20),
        cost_estimate=pl.CostEstimate(flops=4 * HD * work, bytes_accessed=8 * 2**20, transcendentals=work),
    )(table, valid, lanes, *operands)


def attend(table, valid, lanes, own, other):
    state = attend_call(table, valid, lanes, own, None, ())
    return attend_call(table, valid, lanes, own, other, state)


def plan(order, valid, parity, per_group, table):
    groups = order.shape[0]
    for j in range(groups):
        table[PLACE + order[j]] = j
    starts = [jnp.int32(0), jnp.int32(0)]
    gaps = [jnp.int32(0), jnp.int32(0)]
    held = jnp.int32(0)
    for j in range(groups):
        held = held + jnp.right_shift(jnp.right_shift(valid[j] + ROWS - 1, SHIFT) + 1 - parity, 1)
    tiles = lax.div(held + TILE - 1, jnp.int32(TILE))
    pad = tiles * TILE - held
    table[TILES], table[PAD] = tiles, pad
    filled = pad
    for p in range(groups):
        j = table[PLACE + p]
        blocks = jnp.right_shift(valid[j] + ROWS - 1, SHIFT)
        gap = blocks * ROWS - valid[j]
        last_core = jnp.bitwise_and(blocks - 1, 1)
        counts = [jnp.right_shift(blocks + 1 - core, 1) for core in (parity, 1 - parity)]
        for which, core in enumerate((parity, 1 - parity)):
            table[STARTS[which] + p] = starts[which]
            starts[which] = starts[which] + counts[which]
            gaps[which] = gaps[which] + jnp.where(last_core == core, gap, 0)
        for i in range(per_group):
            at = filled + i
            table[SLOT + at] = j * per_group + i
            table[LEFT + at] = valid[j] - (2 * i + parity) * ROWS
            table[RANK + at] = p
            for which in range(2):
                table[END[which] + at] = starts[which]
                table[GAP[which] + at] = gaps[which]
        filled = filled + counts[0]
    for which in range(2):
        table[STARTS[which] + groups] = starts[which]
    for i in range(TILE):
        front = i < pad
        table[SLOT + i] = jnp.where(front, table[SLOT + pad], table[SLOT + i])
        table[LEFT + i] = jnp.where(front, 0, table[LEFT + i])
        table[RANK + i] = jnp.where(front, table[RANK + pad], table[RANK + i])
        for base in (*END, *GAP):
            table[base + i] = jnp.where(front, table[base + pad], table[base + i])


def describe_tiles(table, lanes):
    def describe(tile, carry):
        for i in range(TILE):
            for n, base in enumerate((END[0], END[1], GAP[0], GAP[1], LEFT, RANK)):
                of_block = jnp.full((1, ROWS), table[base + tile * TILE + i], jnp.int32)
                lanes[tile, n : n + 1, i * ROWS : (i + 1) * ROWS] = of_block
        return carry

    lax.fori_loop(0, table[TILES], describe, 0)


def split_kernel(heads, order, valid, query_rows, key_rows, value_rows, out, table_out, lanes_out, *scratch):
    staged, order_here, valid_here, table, lanes, taken, given, read, written = scratch
    inputs = (query_rows, key_rows, value_rows)
    small = [
        pltpu.make_async_copy(order, order_here, read.at[0]),
        pltpu.make_async_copy(valid, valid_here, read.at[1]),
    ]
    arrivals = [pltpu.make_async_copy(rows.at[0], staged.at[n], taken.at[n]) for n, rows in enumerate(inputs)]
    for copy in (*small, *arrivals):
        copy.start()
    for copy in small:
        copy.wait()
    slots = out.shape[0]
    parity = jnp.bitwise_and(lax.axis_index("head"), 1)
    chip = (lax.axis_index("group") * lax.axis_size("head") + lax.axis_index("head") - parity) // 2
    table[PARITY], table[ACTIVE] = parity, (chip < heads).astype(jnp.int32)
    plan(order_here, valid_here, parity, slots // order.shape[0], table)
    table_gone = pltpu.make_async_copy(table, table_out, written.at[0])
    table_gone.start()
    for n, copy in enumerate(arrivals):
        copy.wait()
        for h in range(heads):
            pltpu.make_async_copy(
                staged.at[n, :, h * HD : (h + 1) * HD], out.at[h, n * ROWS : (n + 1) * ROWS], given
            ).start()
    describe_tiles(table, lanes)
    lanes_gone = pltpu.make_async_copy(lanes, lanes_out, written.at[1])
    lanes_gone.start()
    everything = out.at[0:heads]
    pltpu.make_async_copy(everything, everything, given).wait()
    table_gone.wait()
    lanes_gone.wait()


def split_heads(slots, order, valid, query_rows, key_rows, value_rows):
    hbm = pl.BlockSpec(memory_space=pltpu.HBM)
    return pl.pallas_call(
        functools.partial(split_kernel, query_rows.shape[2] // HD),
        out_shape=(
            jax.ShapeDtypeStruct((slots, 3 * ROWS, HD), query_rows.dtype),
            jax.ShapeDtypeStruct((SIZE,), jnp.int32),
            jax.ShapeDtypeStruct((pl.cdiv(slots, TILE), 8, LANES), jnp.int32),
        ),
        in_specs=[hbm] * 5,
        out_specs=(hbm,) * 3,
        scratch_shapes=[
            pltpu.VMEM((3, *query_rows.shape[1:]), query_rows.dtype),
            pltpu.SMEM(order.shape, jnp.int32),
            pltpu.SMEM(valid.shape, jnp.int32),
            pltpu.SMEM((SIZE,), jnp.int32),
            pltpu.VMEM((pl.cdiv(slots, TILE), 8, LANES), jnp.int32),
            pltpu.SemaphoreType.DMA((3,)),
            pltpu.SemaphoreType.DMA,
            pltpu.SemaphoreType.DMA((2,)),
            pltpu.SemaphoreType.DMA((2,)),
        ],
        compiler_params=pltpu.CompilerParams(vmem_limit_bytes=61 * 2**20),
    )(order, valid, query_rows, key_rows, value_rows)


def join_kernel(heads, attended, out, sem):
    for h in range(heads):
        pltpu.make_async_copy(attended.at[h], out.at[0, :, h * HD : (h + 1) * HD], sem).start()
    pltpu.make_async_copy(out, out, sem).wait()


def join_heads(heads, attended):
    return pl.pallas_call(
        functools.partial(join_kernel, heads),
        out_shape=jax.ShapeDtypeStruct((1, ROWS, heads * HD), attended.dtype),
        in_specs=[pl.BlockSpec(memory_space=pltpu.VMEM)],
        out_specs=pl.BlockSpec(memory_space=pltpu.HBM),
        scratch_shapes=[pltpu.SemaphoreType.DMA],
        compiler_params=pltpu.CompilerParams(vmem_limit_bytes=8 * 2**20),
    )(attended)


def body(query_rows, key_rows, value_rows, group_order, valid_counts):
    groups, cores = lax.axis_size("group"), lax.axis_size("head")
    devices = groups * cores
    slots = devices // 2
    heads = query_rows.shape[2] // HD
    same_core = [[i for i in range(devices) if i % 2 == core] for core in range(2)]

    def exchange(x):
        return lax.all_to_all(x, ("group", "head"), 0, 0, axis_index_groups=same_core, tiled=True)

    sent, table, lanes = split_heads(slots, group_order, valid_counts, query_rows, key_rows, value_rows)
    own = exchange(sent)
    other = lax.ppermute(own, "head", [(i, i ^ 1) for i in range(cores)])
    attended = attend(table, valid_counts, lanes, own, other)
    return join_heads(heads, exchange(attended))


def solution(mesh):
    placed = (
        P("group", "head", None),
        P("group", "head", None),
        P("group", "head", None),
        P(),
        P(),
    )
    return jax.shard_map(
        body, mesh=mesh, in_specs=placed, out_specs=P("group", "head", None), check_vma=False
    )
```
